32 devices in a mesh: gx: 4 (over y, core), gy: 4 (over z), gz: 2 (over x).
Axes of the slice: x: 2, y: 2, z: 4, core: 2. Of those that a mesh axis runs over, the one named last changes fastest.
Arguments:
- features: bfloat16 [32, 12, 32, 256], P(None, 'gx', 'gy', 'gz'), may hold values from -6 to 6
- edge_state: bfloat16 [3, 32, 12, 32, 256], P(None, None, 'gx', 'gy', 'gz'), may hold values from -6 to 6
- multiplicity: int32 [12, 32, 256], P('gx', 'gy', 'gz'), may hold values from 0 to 8, as said below
- edge_in: bfloat16 [3, 32, 96], replicated, may hold values from -0.625 to 0.625
- edge_out: bfloat16 [3, 32, 32], replicated, may hold values from -1 to 1
- edge_bias: float32 [3, 32], replicated, may hold values from -3 to 3
- node_in: bfloat16 [3, 32, 64], replicated, may hold values from -0.75 to 0.75
- node_out: bfloat16 [3, 32, 32], replicated, may hold values from -1 to 1
- node_bias: float32 [3, 32], replicated, may hold values from -3 to 3
Outputs:
- updated_features: bfloat16 [32, 12, 32, 256], P(None, 'gx', 'gy', 'gz')
The draws below stay inside these ranges and needn't reach their ends.
Inputs may be any that keep to these rules, and one draw needn't show every extreme that they name: multiplicity(n) is the number of fluid blocks that hold a stored copy of node n; copies are the shared outermost layers of adjacent blocks as described in the reference program, and the nodes inside a void block count 0.
All inputs are finite; a program needn't handle non-finite values.
Results may differ from the reference program's by a relative error of at most 0.009.
Values sent between devices are 32-bit elements; how exact they have to be, the bound alone decides.
A program may use at most 64 MiB of HBM per device.

```python
import jax
import jax.numpy as jnp
from jax import lax

H = 32
LAYERS = 3
CX = 3
CY = 8
CZ = 128
NX = 12
NY = 32
NZ = 256


def members(cells, width, blocks):
    position = jnp.arange(cells)[:, None]
    owner = position // width
    local_pos = position % width
    block_ids = jnp.arange(blocks)[None, :]
    held = (block_ids == owner) | (local_pos == width - 1) & (block_ids == owner + 1) | (local_pos == 0) & (block_ids == owner - 1)
    return held.astype(jnp.int32)


def draw_multiplicity(key, part):
    blocks_x, blocks_y, blocks_z = (NX // CX, NY // CY, NZ // CZ)
    chance = jax.random.randint(jax.random.fold_in(key, 11), (blocks_x, blocks_y, blocks_z), 0, 4)
    fluid = (chance < 3).astype(jnp.int32)
    index_x = jnp.arange(blocks_x)[:, None, None]
    index_y = jnp.arange(blocks_y)[None, :, None]
    index_z = jnp.arange(blocks_z)[None, None, :]
    corner = ((index_x < 2) & (index_y < 2) & (index_z < 2)).astype(jnp.int32)
    far_block = (index_x == blocks_x - 1) & (index_y == blocks_y - 1) & (index_z == blocks_z - 1)
    fluid = jnp.where(far_block, 0, jnp.maximum(fluid, corner)).astype(jnp.int32)
    held_x = members(NX, CX, blocks_x)
    held_y = members(NY, CY, blocks_y)
    held_z = members(NZ, CZ, blocks_z)
    return jnp.einsum('xa,yb,zc,abc->xyz', held_x, held_y, held_z, fluid).astype(jnp.int32)


def steps_of(stream_key, shape, cuts, smallest, largest):
    level, own = 1.0, jax.random.fold_in(stream_key, 6)
    for dim, parts in cuts:
        heights = jnp.exp(jax.random.uniform(jax.random.fold_in(own, dim), (parts,), jnp.float32, smallest / len(cuts), largest / len(cuts)))
        level = level * jnp.repeat(heights, shape[dim] // parts).reshape([-1 if axis == dim else 1 for axis in range(len(shape))])
    return level


def scatter_about(own_key, shape, scale, limit, pieces=(), dtype=jnp.bfloat16):
    values = jax.random.normal(own_key, shape, jnp.float32) * scale
    if len(pieces) > 0:
        values = steps_of(own_key, shape, pieces, -0.22, 0.18) * values
    return jnp.clip(values, min=-limit, max=limit).astype(dtype)


def setup_inputs(seed: int = 0) -> dict:
    arg_keys = jax.random.split(jax.random.key(seed), 10)
    return {
        "features": scatter_about(arg_keys[0], (H, NX, NY, NZ), 1.0, 6.0, ((1, 4), (2, 4), (3, 2))),
        "edge_state": scatter_about(arg_keys[1], (3, H, NX, NY, NZ), 1.0, 6.0, ((2, 4), (3, 4), (4, 2))),
        "multiplicity": draw_multiplicity(jax.random.fold_in(arg_keys[9], 71), 0),
        "edge_in": scatter_about(arg_keys[3], (LAYERS, H, 3 * H), (3 * H) ** -0.5, 0.625),
        "edge_out": scatter_about(arg_keys[4], (LAYERS, H, H), H ** -0.5, 1.0),
        "edge_bias": scatter_about(arg_keys[5], (LAYERS, H), 0.5, 3.0, (), jnp.float32),
        "node_in": scatter_about(arg_keys[6], (LAYERS, H, 2 * H), (2 * H) ** -0.5, 0.75),
        "node_out": scatter_about(arg_keys[7], (LAYERS, H, H), H ** -0.5, 1.0),
        "node_bias": scatter_about(arg_keys[8], (LAYERS, H), 0.5, 3.0, (), jnp.float32),
    }


def ahead(values, axis_pos):
    length = values.shape[axis_pos]
    remainder = lax.slice_in_dim(values, 1, length, axis=axis_pos)
    filler = jnp.zeros_like(lax.slice_in_dim(values, 0, 1, axis=axis_pos))
    return jnp.concatenate([remainder, filler], axis=axis_pos)


def behind(values, axis_pos):
    length = values.shape[axis_pos]
    remainder = lax.slice_in_dim(values, 0, length - 1, axis=axis_pos)
    filler = jnp.zeros_like(lax.slice_in_dim(values, 0, 1, axis=axis_pos))
    return jnp.concatenate([filler, remainder], axis=axis_pos)


def edge_layer(hidden_nodes, edges, counts, fluid, weight_in, weight_out, bias_in, spatial, count_dims):
    channels = hidden_nodes.shape[0]
    shape = hidden_nodes.shape
    flat = hidden_nodes.reshape(channels, -1)
    stacked = jnp.concatenate([weight_in[:, :channels], weight_in[:, channels:2 * channels]], axis=0)
    projected = jnp.dot(stacked, flat, preferred_element_type=jnp.float32)
    own_part = projected[:channels].reshape(shape)
    other_part = projected[channels:].reshape(shape)
    bias = bias_in.astype(jnp.float32).reshape((channels,) + (1,) * (hidden_nodes.ndim - 1))
    incoming = jnp.zeros(shape, jnp.float32)
    updated = []
    for direction in range(3):
        edge_now = edges[direction]
        edge_term = jnp.dot(weight_in[:, 2 * channels:], edge_now.reshape(channels, -1), preferred_element_type=jnp.float32).reshape(shape)
        preact = own_part + ahead(other_part, spatial[direction]) + edge_term + bias
        edge_hidden = jax.nn.silu(preact).astype(jnp.bfloat16)
        message = jnp.dot(weight_out, edge_hidden.reshape(channels, -1), preferred_element_type=jnp.float32).reshape(shape)
        updated.append((edge_now + message).astype(jnp.bfloat16))
        shared_count = jnp.minimum(counts, ahead(counts, count_dims[direction]))
        weight_edge = jnp.where(fluid & (shared_count > 0), 1.0 / jnp.maximum(shared_count, 1).astype(jnp.float32), 0.0).astype(jnp.float32)
        weighted = weight_edge[None] * message
        incoming = incoming + weighted + behind(weighted, spatial[direction])
    return incoming, jnp.stack(updated)


def node_layer(hidden_nodes, incoming_rounded, weight_in, weight_out, bias_in):
    channels = hidden_nodes.shape[0]
    shape = hidden_nodes.shape
    node_pre = jnp.dot(weight_in[:, :channels], hidden_nodes.reshape(channels, -1), preferred_element_type=jnp.float32)
    node_pre = node_pre + jnp.dot(weight_in[:, channels:], incoming_rounded.reshape(channels, -1), preferred_element_type=jnp.float32)
    node_pre = node_pre + bias_in.astype(jnp.float32)[:, None]
    node_hidden = jax.nn.silu(node_pre).astype(jnp.bfloat16)
    result = jnp.dot(weight_out, node_hidden, preferred_element_type=jnp.float32).reshape(shape)
    return (hidden_nodes + result).astype(jnp.bfloat16)


def copy_sums(values, block_axis, local_axis):
    width = values.shape[local_axis]
    head_part = lax.index_in_dim(values, 0, local_axis, keepdims=False)
    tail_part = lax.index_in_dim(values, width - 1, local_axis, keepdims=False)
    front = (slice(None),) * local_axis
    return values.at[front + (0,)].add(behind(tail_part, block_axis)).at[front + (width - 1,)].add(ahead(head_part, block_axis))


def reference(features, edge_state, multiplicity, edge_in, edge_out, edge_bias, node_in, node_out, node_bias):
    blocks_x, blocks_y, blocks_z = NX // CX, NY // CY, NZ // CZ

    def to_slabs(values):
        lead = values.ndim - 3
        shaped = values.reshape(values.shape[:lead] + (blocks_x, CX, blocks_y, CY, blocks_z, CZ))
        return jnp.moveaxis(shaped, lead, 0)

    counts = to_slabs(multiplicity)
    fluid = (counts[:, 1, :, 1, :, 1] > 0).reshape(blocks_x, 1, blocks_y, 1, blocks_z, 1)
    hidden_nodes = to_slabs(features)
    edges = to_slabs(edge_state)
    for layer_index in range(LAYERS):
        def per_slab(items):
            return edge_layer(items[0], items[1], items[2], items[3], edge_in[layer_index], edge_out[layer_index], edge_bias[layer_index], (1, 3, 5), (0, 2, 4))

        incoming, edges = lax.map(per_slab, (hidden_nodes, edges, counts, fluid))
        incoming = copy_sums(copy_sums(copy_sums(incoming, 0, 2), 3, 4), 5, 6)
        incoming_rounded = incoming.astype(jnp.bfloat16)

        def per_node_slab(items):
            return node_layer(items[0], items[1], node_in[layer_index], node_out[layer_index], node_bias[layer_index])

        hidden_nodes = lax.map(per_node_slab, (hidden_nodes, incoming_rounded))
    result = jnp.moveaxis(hidden_nodes, 0, 1)
    return result.reshape(result.shape[0], NX, NY, NZ)
```

```python
import functools
import itertools

import jax
import jax.numpy as jnp
from jax import lax
from jax.experimental import pallas as pl
from jax.experimental.pallas import tpu as pltpu
from jax.sharding import PartitionSpec as P

MESH = pl.DeviceIdType.MESH
AXES = ("gx", "gy", "gz")
F32, BF16 = jnp.float32, jnp.bfloat16
WAYS = [way for way in itertools.product((-1, 0, 1), repeat=3) if any(way)]


def iota(shape, dim):
    return lax.broadcasted_iota(jnp.int32, shape, dim)


def dot(a, b):
    return jnp.dot(a, b, preferred_element_type=F32)


def silu_of_half(half):
    return half + half * jnp.tanh(half)


def split(values):
    high = values.astype(BF16)
    return high, (values - high.astype(F32)).astype(BF16)


def kernel(
    sizes,
    layers,
    feat_ref, edge_ref, mult_ref, win_ref, wout_ref, bin_ref, nin_ref, nout_ref, bnode_ref,
    out_ref,
    h_s, hz_s, e_s, w_s, p_s, inc_s, mat_e, mat_o, mat_n, mat_no, bias_e, bias_n,
    ysend, zsend, xrx, yrx, xyrx, zrx, send_sem, recv_sem,
):
    chans, cx, cy, cz = feat_ref.shape
    rows = chans * cy
    halves = rows // 128
    last = cx - 1
    slots = p_s.shape[0]
    zrows = zsend.shape[2]
    place = [lax.axis_index(axis) for axis in AXES]

    def exists(way):
        there = None
        for pos, step, size in zip(place, way, sizes):
            if step == 0:
                continue
            here = pos > 0 if step < 0 else pos < size - 1
            there = here if there is None else there & here
        return there

    def device(way):
        return {axis: pos + step for axis, pos, step in zip(AXES, place, way)}

    def back(way):
        return tuple(-step for step in way)

    ways = [way for way in WAYS if all(step == 0 or size > 1 for step, size in zip(way, sizes))]

    xrx[...] = jnp.zeros_like(xrx)
    yrx[...] = jnp.zeros_like(yrx)
    xyrx[...] = jnp.zeros_like(xyrx)
    zrx[...] = jnp.zeros_like(zrx)

    barrier = pltpu.get_barrier_semaphore()
    for way in ways:
        @pl.when(exists(way))
        def _():
            pl.semaphore_signal(barrier, inc=1, device_id=device(way), device_id_type=MESH)

    spread = (iota((rows, chans), 0) // cy == iota((rows, chans), 1)).astype(F32).astype(BF16)
    row_y, col_y = iota((rows, rows), 0) % cy, iota((rows, rows), 1) % cy
    same_y, next_y = row_y == col_y, row_y + 1 == col_y

    def widen(tall, part):
        width = tall.shape[1]
        pick = iota((width, rows), 0) == part * chans + iota((width, rows), 1) // cy
        return dot(tall, pick.astype(F32).astype(BF16))

    def build(layer):
        tall = dot(spread, win_ref[layer]).astype(BF16)
        own, other, edge = (0.5 * widen(tall, part) for part in range(3))
        own = jnp.where(same_y, own, 0.0)
        mat_e[layer, :, 0:rows] = own.astype(BF16)
        mat_e[layer, :, rows : 2 * rows] = jnp.where(same_y, other, 0.0).astype(BF16)
        mat_e[layer, :, 2 * rows : 3 * rows] = jnp.where(same_y, edge, 0.0).astype(BF16)
        mat_e[layer, :, 3 * rows :] = jnp.where(next_y, other, own).astype(BF16)
        tall = dot(spread, wout_ref[layer]).astype(BF16)
        mat_o[layer] = jnp.where(same_y, widen(tall, 0), 0.0).astype(BF16)
        tall = dot(spread, nin_ref[layer]).astype(BF16)
        for part in range(2):
            mat_n[layer, :, part * rows : (part + 1) * rows] = jnp.where(
                same_y, 0.5 * widen(tall, part), 0.0
            ).astype(BF16)
        tall = dot(spread, nout_ref[layer]).astype(BF16)
        mat_no[layer] = jnp.where(same_y, widen(tall, 0), 0.0).astype(BF16)
        mine = iota((rows, chans), 0) // cy == iota((rows, chans), 1)
        for source, target in ((bin_ref, bias_e), (bnode_ref, bias_n)):
            column = jnp.sum(
                jnp.where(mine, source[pl.ds(layer, 1), :], 0.0), axis=1, keepdims=True
            )
            target[layer] = jnp.broadcast_to(0.5 * column, (rows, cz))

    def build_step(layer, carry):
        build(layer)
        return carry

    lax.fori_loop(0, layers, build_step, 0)

    fluid = mult_ref[1, 1:2, 1:2] > 0
    zeros = jnp.zeros((cy, cz), jnp.int32)
    for x in range(cx):
        count = mult_ref[x]
        ahead = (
            mult_ref[x + 1] if x < last else zeros,
            jnp.where(iota((cy, cz), 0) < cy - 1, pltpu.roll(count, cy - 1, 0), 0),
            jnp.where(iota((cy, cz), 1) < cz - 1, pltpu.roll(count, cz - 1, 1), 0),
        )
        for d in range(3):
            shared = jnp.minimum(count, ahead[d])
            w_s[d, x] = jnp.where(
                fluid & (shared > 0), 1.0 / jnp.maximum(shared, 1).astype(F32), 0.0
            )

    before_end = iota((rows, cz), 1) < cz - 1

    def keep_nodes(x, values):
        h_s[x] = values.astype(BF16)
        hz_s[x] = jnp.where(before_end, pltpu.roll(values, cz - 1, 1), 0.0).astype(BF16)

    for x in range(cx):
        keep_nodes(x, feat_ref[:, x].astype(F32).reshape(rows, cz))
        for d in range(3):
            e_s[d, x] = edge_ref[d, :, x].astype(F32).reshape(rows, cz).astype(BF16)

    def finish(layer, slabs, half):
        count = len(slabs)
        half = half + jnp.concatenate([bias_e[layer]] * count, axis=1)
        message = dot(mat_o[layer], silu_of_half(half).astype(BF16))
        weighted = []
        for index, (x, d) in enumerate(slabs):
            own = message[:, index * cz : (index + 1) * cz]
            e_s[d, x] = (e_s[d, x].astype(F32) + own).astype(BF16)
            weighted.append(w_s[d, x][None] * own.reshape(chans, cy, cz))
        return weighted

    def edges_xz(layer, slabs):
        nothing = jnp.zeros((rows, cz), BF16)
        own = jnp.concatenate([h_s[x] for x, d in slabs], axis=1)
        other = jnp.concatenate(
            [hz_s[x] if d == 2 else h_s[x + 1] if x < last else nothing for x, d in slabs], axis=1
        )
        edge = jnp.concatenate([e_s[d, x] for x, d in slabs], axis=1)
        stacked = jnp.concatenate([own, other, edge], axis=0)
        return finish(layer, slabs, dot(mat_e[layer, :, 0 : 3 * rows], stacked))

    def edges_y(layer, xs):
        edge = jnp.concatenate([e_s[1, x] for x in xs], axis=1)
        own = jnp.concatenate([h_s[x] for x in xs], axis=1)
        stacked = jnp.concatenate([edge, own], axis=0)
        slabs = [(x, 1) for x in xs]
        return finish(layer, slabs, dot(mat_e[layer, :, 2 * rows :], stacked))

    def both_y(weighted):
        return weighted + pltpu.roll(weighted, 1, 1)

    def both_z(weighted):
        return weighted + pltpu.roll(weighted, 1, 2)

    def put(slot, x, value, add):
        value = value.reshape(rows, cz)
        if add:
            value = p_s[slot, x] + value
        p_s[slot, x] = value

    def transfer(way, slot):
        dx, dy, dz = way
        side = 0 if dy < 0 else 1
        face = 0 if dx < 0 else last
        if dz != 0:
            source = zsend.at[slot, 0 if dz < 0 else 1]
            target = zrx.at[slot, (dx + 1) * 6 + (dy + 1) * 2 + (0 if dz < 0 else 1)]
        elif dy == 0:
            source = p_s.at[slot, face]
            target = xrx.at[slot, 0 if dx < 0 else 1]
        elif dx == 0:
            source = ysend.at[slot, side]
            target = yrx.at[slot, side]
        else:
            source = ysend.at[slot, side, face]
            target = xyrx.at[slot, (0 if dx < 0 else 2) + side]
        index = WAYS.index(way)
        return pltpu.make_async_remote_copy(
            src_ref=source,
            dst_ref=target,
            send_sem=send_sem.at[slot, index],
            recv_sem=recv_sem.at[slot, index],
            device_id=device(way),
            device_id_type=MESH,
        )

    def start(way, slot):
        @pl.when(exists(way))
        def _():
            transfer(way, slot).start()

    def arrive(way, slot):
        @pl.when(exists(back(way)))
        def _():
            transfer(way, slot).wait_recv()

    def sent(way, slot):
        @pl.when(exists(way))
        def _():
            transfer(way, slot).wait_send()

    x_ways = [way for way in ways if way[1] == 0 and way[2] == 0]
    y_ways = [way for way in ways if way[1] != 0 and way[2] == 0]
    z_ways = [way for way in ways if way[2] != 0]

    z_row, z_lane = iota((2 * zrows, 128), 0), iota((2 * zrows, 128), 1)

    def z_faces(slot):
        faces = jnp.zeros((2 * zrows, 128), F32)
        for x in range(cx):
            for part in range(halves):
                high, low = split(p_s[slot, x, part * 128 : (part + 1) * 128])
                at = x * halves + part
                pick = ((z_row == at) & (z_lane == 0)) | (
                    (z_row == zrows + at) & (z_lane == cz - 1)
                )
                pick = pick.astype(F32).astype(BF16)
                for piece in (high, low):
                    faces = faces + lax.dot_general(
                        pick, piece, (((1,), (1,)), ((), ())), preferred_element_type=F32
                    )
        zsend[slot, 0] = faces[:zrows]
        zsend[slot, 1] = faces[zrows:]

    row_z, lane_z = iota((zrows, 128), 0), iota((zrows, 128), 1)

    def z_total(slot, dz):
        total = jnp.zeros((zrows, 128), F32)
        shift_x, shift_y = last * halves, cy - 1
        for dy in (-1, 0, 1):
            part = jnp.zeros((zrows, 128), F32)
            for dx in (-1, 0, 1):
                piece = zrx[slot, (dx + 1) * 6 + (dy + 1) * 2 + (0 if dz < 0 else 1)]
                if dx > 0:
                    piece = jnp.where(row_z < halves, pltpu.roll(piece, zrows - shift_x, 0), 0.0)
                if dx < 0:
                    inside = (row_z >= shift_x) & (row_z < shift_x + halves)
                    piece = jnp.where(inside, pltpu.roll(piece, shift_x, 0), 0.0)
                part = part + piece
            if dy > 0:
                part = jnp.where(lane_z % cy == 0, pltpu.roll(part, 128 - shift_y, 1), 0.0)
            if dy < 0:
                part = jnp.where(lane_z % cy == cy - 1, pltpu.roll(part, shift_y, 1), 0.0)
            total = total + part
        return total

    def z_columns(slot):
        both = jnp.concatenate(
            [z_total(slot, 1), z_total(slot, -1), jnp.zeros((128 - 2 * zrows, 128), F32)], axis=0
        )
        high, low = split(both.T)
        return jnp.concatenate([high, low], axis=1)

    place_row, place_lane = iota((256, cz), 0) % 128, iota((256, cz), 1)

    def z_add(columns, x):
        out = []
        for part in range(halves):
            at = x * halves + part
            pick = ((place_row == at) & (place_lane == 0)) | (
                (place_row == zrows + at) & (place_lane == cz - 1)
            )
            out.append(dot(columns, pick.astype(F32).astype(BF16)))
        return jnp.concatenate(out, axis=0)

    def y_rows(side):
        return pl.ds(0 if side == 0 else cy - 1, chans, stride=cy)

    def node(layer, slot, x, columns):
        total = p_s[slot, x] + z_add(columns, x)
        if x == 0:
            total = total + xrx[slot, 1]
        if x == last:
            total = total + xrx[slot, 0]
        inc_s[x] = total
        for side in range(2):
            extra = yrx[slot, 1 - side, x]
            if x == 0:
                extra = extra + xyrx[slot, 2 + (1 - side)]
            if x == last:
                extra = extra + xyrx[slot, 1 - side]
            inc_s[x, y_rows(side), :] = inc_s[x, y_rows(side), :] + extra
        stacked = jnp.concatenate([h_s[x], inc_s[x].astype(BF16)], axis=0)
        half = dot(mat_n[layer], stacked) + bias_n[layer]
        step = dot(mat_no[layer], silu_of_half(half).astype(BF16))
        return (h_s[x].astype(F32) + step).astype(BF16).astype(F32)

    middle = list(range(1, last))

    def middle_edges(layer, slot):
        for x in middle:
            (wz,) = edges_xz(layer, [(x, 2)])
            (wy,) = edges_y(layer, [x])
            put(slot, x, both_z(wz) + both_y(wy), False)

    middle_edges(0, 0)
    pl.semaphore_wait(
        barrier,
        functools.reduce(
            lambda a, b: a * b,
            [
                1 + (pos > 0).astype(jnp.int32) + (pos < size - 1).astype(jnp.int32)
                for pos, size in zip(place, sizes)
            ],
        )
        - 1,
    )

    def layer_step(layer, carry):
        slot = lax.rem(layer, slots)
        after = lax.rem(layer + 1, slots)
        w0, wz = edges_xz(layer, [(0, 0), (0, 2)])
        (wy,) = edges_y(layer, [0])
        put(slot, 0, w0 + both_z(wz) + both_y(wy), False)
        for way in x_ways:
            if way[0] < 0:
                start(way, slot)
        ring = [(x, 0) for x in range(1, cx)]
        *wx, wz = edges_xz(layer, ring + [(last, 2)])
        (wy,) = edges_y(layer, [last])
        wx = [w0] + wx
        put(slot, last, wx[last - 1] + wx[last] + both_z(wz) + both_y(wy), False)
        for way in x_ways:
            if way[0] > 0:
                start(way, slot)
        for x in middle:
            put(slot, x, wx[x - 1] + wx[x], True)
        for side in range(2):
            for x in range(cx):
                ysend[slot, side, x] = p_s[slot, x, y_rows(side), :]
        for way in y_ways:
            start(way, slot)
        z_faces(slot)
        for way in z_ways:
            start(way, slot)
        for way in y_ways + z_ways:
            arrive(way, slot)
        columns = z_columns(slot)
        for x in middle:
            keep_nodes(x, node(layer, slot, x, columns))

        @pl.when(layer + 1 < layers)
        def _():
            middle_edges(layer + 1, after)

        for way in x_ways:
            arrive(way, slot)
        keep_nodes(0, node(layer, slot, 0, columns))
        keep_nodes(last, node(layer, slot, last, columns))
        for way in ways:
            sent(way, slot)
        return carry

    lax.fori_loop(0, layers, layer_step, 0)
    for x in range(cx):
        out_ref[:, x] = h_s[x].astype(F32).reshape(chans, cy, cz).astype(BF16)


def solution(mesh):
    sizes = tuple(mesh.shape[axis] for axis in AXES)

    def on_device(features, edge_state, multiplicity, *params):
        layers = params[0].shape[0]
        chans, cx, cy, cz = features.shape
        rows = chans * cy
        assert cz == 128 and rows % 128 == 0 and cy % 8 == 0 and cx > 1
        slots = min(layers, 2)
        zrows = -(-cx * (rows // 128) // 8) * 8
        vmem = pl.BlockSpec(memory_space=pltpu.VMEM)
        scratch = [
            pltpu.VMEM((cx, rows, cz), BF16),
            pltpu.VMEM((cx, rows, cz), BF16),
            pltpu.VMEM((3, cx, rows, cz), BF16),
            pltpu.VMEM((3, cx, cy, cz), F32),
            pltpu.VMEM((slots, cx, rows, cz), F32),
            pltpu.VMEM((cx, rows, cz), F32),
            pltpu.VMEM((layers, rows, 4 * rows), BF16),
            pltpu.VMEM((layers, rows, rows), BF16),
            pltpu.VMEM((layers, rows, 2 * rows), BF16),
            pltpu.VMEM((layers, rows, rows), BF16),
            pltpu.VMEM((layers, rows, cz), F32),
            pltpu.VMEM((layers, rows, cz), F32),
            pltpu.VMEM((slots, 2, cx, chans, cz), F32),
            pltpu.VMEM((slots, 2, zrows, 128), F32),
            pltpu.VMEM((slots, 2, rows, cz), F32),
            pltpu.VMEM((slots, 2, cx, chans, cz), F32),
            pltpu.VMEM((slots, 4, chans, cz), F32),
            pltpu.VMEM((slots, 18, zrows, 128), F32),
            pltpu.SemaphoreType.DMA((slots, len(WAYS))),
            pltpu.SemaphoreType.DMA((slots, len(WAYS))),
        ]
        return pl.pallas_call(
            functools.partial(kernel, sizes, layers),
            out_shape=jax.ShapeDtypeStruct(features.shape, features.dtype),
            in_specs=[vmem] * 9,
            out_specs=vmem,
            scratch_shapes=scratch,
            compiler_params=pltpu.CompilerParams(
                collective_id=0, has_side_effects=True, vmem_limit_bytes=48 * 1024 * 1024
            ),
        )(features, edge_state, multiplicity, *params)

    placed = (P(None, *AXES), P(None, None, *AXES), P(*AXES)) + (P(),) * 6
    return jax.shard_map(
        on_device, mesh=mesh, in_specs=placed, out_specs=P(None, *AXES), check_vma=False
    )
```

```python
import functools
import itertools

import jax
import jax.numpy as jnp
from jax import lax
from jax.experimental import pallas as pl
from jax.experimental.pallas import tpu as pltpu
from jax.sharding import PartitionSpec as P

MESH = pl.DeviceIdType.MESH
AXES = ("gx", "gy", "gz")
F32, BF16 = jnp.float32, jnp.bfloat16
STEPS = (-1, 0, 1)
OTHER = 2


def iota(shape, dim):
    return lax.broadcasted_iota(jnp.int32, shape, dim)


def dot(a, b):
    return jnp.dot(a, b, preferred_element_type=F32)


def silu_of_half(half):
    return half + half * jnp.tanh(half)


def ways_of(sizes):
    z_steps = {1: (0,), 2: (0, OTHER)}.get(sizes[2], STEPS)
    ways = itertools.product(STEPS, STEPS, z_steps)
    return [
        way for way in ways if any(way) and all(s == 0 or n > 1 for s, n in zip(way, sizes))
    ]


def kernel(
    sizes,
    layers,
    feat_hbm, edge_hbm, mult_hbm, win_hbm, wout_hbm, bin_hbm, nin_hbm, nout_hbm, bnode_hbm,
    out_ref,
    feat_ref, edge_ref, mult_ref, win_ref, wout_ref, bin_ref, nin_ref, nout_ref, bnode_ref,
    h_s, hz_s, e_s, w_s, p_s, inc_s, mat_e, mat_o, mat_n, mat_no, bias_e, bias_n,
    ysend, zsend, xrx, yrx, xyrx, zrx, turn_s, in_sem, send_sem, recv_sem,
):
    loads = [
        pltpu.make_async_copy(source, target, in_sem.at[index])
        for index, (source, target) in enumerate([
            (win_hbm, win_ref), (wout_hbm, wout_ref), (bin_hbm, bin_ref), (nin_hbm, nin_ref),
            (nout_hbm, nout_ref), (bnode_hbm, bnode_ref), (mult_hbm, mult_ref),
            (feat_hbm, feat_ref), (edge_hbm, edge_ref),
        ])
    ]
    for load in loads:
        load.start()

    chans, cx, cy, cz = feat_ref.shape
    rows = chans * cy
    halves = rows // 128
    last = cx - 1
    zrows = zsend.shape[2]
    place = [lax.axis_index(axis) for axis in AXES]

    def exists(way):
        there = None
        for pos, step, size in zip(place, way, sizes):
            if step == 0 or step == OTHER:
                continue
            here = pos > 0 if step < 0 else pos < size - 1
            there = here if there is None else there & here
        return there

    def device(way):
        return {
            axis: 1 - pos if step == OTHER else pos + step
            for axis, pos, step in zip(AXES, place, way)
        }

    def back(way):
        return tuple(step if step == OTHER else -step for step in way)

    def when_exists(way, act):
        there = exists(way)
        if there is None:
            act()
        else:
            pl.when(there)(act)

    ways = ways_of(sizes)
    z_steps = [way[2] for way in ways if way[0] == 0 and way[1] == 0 and way[2] != 0]

    xrx[...] = jnp.zeros_like(xrx)
    yrx[...] = jnp.zeros_like(yrx)
    xyrx[...] = jnp.zeros_like(xyrx)
    zrx[...] = jnp.zeros_like(zrx)

    barrier = pltpu.get_barrier_semaphore()
    for way in ways:
        def greet(way=way):
            pl.semaphore_signal(barrier, inc=1, device_id=device(way), device_id_type=MESH)

        when_exists(way, greet)

    mine = iota((rows, chans), 0) // cy == iota((rows, chans), 1)
    spread = mine.astype(F32).astype(BF16)
    row_y, col_y = iota((cy, rows), 0), iota((cy, rows), 1) % cy
    same_y = (row_y == col_y).astype(F32)
    half_same, half_next = 0.5 * same_y, 0.5 * (row_y + 1 == col_y).astype(F32)
    col_c = iota((1, rows), 1) // cy

    def widen(weights):
        width = weights.shape[1]
        parts = []
        for part in range(width // chans):
            pick = iota((width, rows), 0) == part * chans + col_c
            parts.append(dot(weights, pick.astype(F32).astype(BF16)).astype(BF16))
        return parts

    def build(layer):
        wide = widen(win_ref[layer]) + widen(wout_ref[layer])
        wide += widen(nin_ref[layer]) + widen(nout_ref[layer])

        def block(index):
            return dot(spread, wide[index]).reshape(chans, cy, rows)

        def flat(values):
            return values.reshape(rows, rows).astype(BF16)

        own, other = block(0), block(1)
        own_same = own * half_same[None]
        mat_e[layer, :, 0:rows] = flat(own_same)
        mat_e[layer, :, rows : 2 * rows] = flat(other * half_same[None])
        mat_e[layer, :, 2 * rows : 3 * rows] = flat(block(2) * half_same[None])
        mat_e[layer, :, 3 * rows :] = flat(own_same + other * half_next[None])
        mat_o[layer] = flat(block(3) * same_y[None])
        mat_n[layer, :, 0:rows] = flat(block(4) * half_same[None])
        mat_n[layer, :, rows:] = flat(block(5) * half_same[None])
        mat_no[layer] = flat(block(6) * same_y[None])
        for source, target in ((bin_ref, bias_e), (bnode_ref, bias_n)):
            column = jnp.sum(
                jnp.where(mine, source[pl.ds(layer, 1), :], 0.0), axis=1, keepdims=True
            )
            target[layer] = jnp.broadcast_to(0.5 * column, (rows, cz))

    for load in loads[:6]:
        load.wait()
    build(0)
    for load in loads[6:]:
        load.wait()

    fluid = mult_ref[1, 1:2, 1:2] > 0
    zeros = jnp.zeros((cy, cz), jnp.int32)
    for x in range(cx):
        count = mult_ref[x]
        ahead = (
            mult_ref[x + 1] if x < last else zeros,
            jnp.where(iota((cy, cz), 0) < cy - 1, pltpu.roll(count, cy - 1, 0), 0),
            jnp.where(iota((cy, cz), 1) < cz - 1, pltpu.roll(count, cz - 1, 1), 0),
        )
        for d in range(3):
            shared = jnp.minimum(count, ahead[d])
            w_s[d, x] = jnp.where(
                fluid & (shared > 0), 1.0 / jnp.maximum(shared, 1).astype(F32), 0.0
            )

    before_end = iota((rows, cz), 1) < cz - 1

    def keep_nodes(x, values):
        h_s[x] = values.astype(BF16)
        hz_s[x] = jnp.where(before_end, pltpu.roll(values, cz - 1, 1), 0.0).astype(BF16)

    for x in range(cx):
        keep_nodes(x, feat_ref[:, x].astype(F32).reshape(rows, cz))
        for d in range(3):
            e_s[d, x] = edge_ref[d, :, x].astype(F32).reshape(rows, cz).astype(BF16)

    def finish(layer, slabs, half):
        count = len(slabs)
        half = half + jnp.concatenate([bias_e[layer]] * count, axis=1)
        message = dot(mat_o[layer], silu_of_half(half).astype(BF16))
        weighted = []
        for index, (x, d) in enumerate(slabs):
            own = message[:, index * cz : (index + 1) * cz]
            e_s[d, x] = (e_s[d, x].astype(F32) + own).astype(BF16)
            weighted.append(w_s[d, x][None] * own.reshape(chans, cy, cz))
        return weighted

    def edges_xz(layer, slabs):
        nothing = jnp.zeros((rows, cz), BF16)
        own = jnp.concatenate([h_s[x] for x, d in slabs], axis=1)
        other = jnp.concatenate(
            [hz_s[x] if d == 2 else h_s[x + 1] if x < last else nothing for x, d in slabs], axis=1
        )
        edge = jnp.concatenate([e_s[d, x] for x, d in slabs], axis=1)
        stacked = jnp.concatenate([own, other, edge], axis=0)
        return finish(layer, slabs, dot(mat_e[layer, :, 0 : 3 * rows], stacked))

    def edges_y(layer, xs):
        edge = jnp.concatenate([e_s[1, x] for x in xs], axis=1)
        own = jnp.concatenate([h_s[x] for x in xs], axis=1)
        stacked = jnp.concatenate([edge, own], axis=0)
        slabs = [(x, 1) for x in xs]
        return finish(layer, slabs, dot(mat_e[layer, :, 2 * rows :], stacked))

    def both_y(weighted):
        return weighted + pltpu.roll(weighted, 1, 1)

    def both_z(weighted):
        return weighted + pltpu.roll(weighted, 1, 2)

    def put(slot, x, value, add):
        value = value.reshape(rows, cz)
        if add:
            value = p_s[slot, x] + value
        p_s[slot, x] = value

    def transfer(way, slot):
        dx, dy, dz = way
        index = ways.index(way)
        side = 0 if dy < 0 else 1
        face = 0 if dx < 0 else last
        if dz != 0:
            which = z_steps.index(dz)
            source = zsend.at[slot, which]
            target = zrx.at[slot, which, (dx + 1) * 3 + dy + 1]
        elif dy == 0:
            source = p_s.at[slot, face]
            target = xrx.at[slot, 0 if dx < 0 else 1]
        elif dx == 0:
            source = ysend.at[slot, side]
            target = yrx.at[slot, side]
        else:
            source = ysend.at[slot, side, face]
            target = xyrx.at[slot, (0 if dx < 0 else 2) + side]
        return pltpu.make_async_remote_copy(
            src_ref=source,
            dst_ref=target,
            send_sem=send_sem.at[slot, index],
            recv_sem=recv_sem.at[slot, index],
            device_id=device(way),
            device_id_type=MESH,
        )

    def start(way, slot):
        when_exists(way, lambda: transfer(way, slot).start())

    def arrive(way, slot):
        when_exists(back(way), lambda: transfer(way, slot).wait_recv())

    def sent(way, slot):
        when_exists(way, lambda: transfer(way, slot).wait_send())

    x_ways = [way for way in ways if way[1] == 0 and way[2] == 0]
    y_ways = [way for way in ways if way[1] != 0 and way[2] == 0]
    z_ways = [way for way in ways if way[2] != 0]

    lane = iota((128, cz), 1)
    odd_rows, even_rows = pl.ds(1, zrows, stride=2), pl.ds(0, zrows, stride=2)

    def z_faces(slot):
        faces = jnp.zeros((128, cz), F32)
        for x in range(cx):
            for part in range(halves):
                at = 2 * (x * halves + part)
                piece = pltpu.roll(p_s[slot, x, part * 128 : (part + 1) * 128], at + 1, 1)
                faces = jnp.where((lane == at) | (lane == at + 1), piece, faces)
        turn_s[0] = faces.T
        first, final = turn_s[0, odd_rows, :], turn_s[0, even_rows, :]
        for which, dz in enumerate(z_steps):
            if dz == OTHER:
                zsend[slot, which] = jnp.where(place[2] == 0, final, first)
            else:
                zsend[slot, which] = first if dz < 0 else final

    row_z, lane_z = iota((zrows, 128), 0), iota((zrows, 128), 1)

    def z_total(slot, which):
        total = jnp.zeros((zrows, 128), F32)
        shift_x, shift_y = last * halves, cy - 1
        for dy in (-1, 0, 1):
            part = jnp.zeros((zrows, 128), F32)
            for dx in (-1, 0, 1):
                piece = zrx[slot, which, (dx + 1) * 3 + dy + 1]
                if dx > 0:
                    piece = jnp.where(row_z < halves, pltpu.roll(piece, zrows - shift_x, 0), 0.0)
                if dx < 0:
                    inside = (row_z >= shift_x) & (row_z < shift_x + halves)
                    piece = jnp.where(inside, pltpu.roll(piece, shift_x, 0), 0.0)
                part = part + piece
            if dy > 0:
                part = jnp.where(lane_z % cy == 0, pltpu.roll(part, 128 - shift_y, 1), 0.0)
            if dy < 0:
                part = jnp.where(lane_z % cy == cy - 1, pltpu.roll(part, shift_y, 1), 0.0)
            total = total + part
        return total

    def z_columns(slot):
        for which, dz in enumerate(z_steps):
            total = z_total(slot, which)
            if dz != 1:
                turn_s[1, even_rows, :] = jnp.where(place[2] < sizes[2] - 1, total, 0.0)
            if dz != -1:
                turn_s[1, odd_rows, :] = jnp.where(place[2] > 0, total, 0.0)
        return turn_s[1].T

    def z_add(columns, x):
        out = []
        for part in range(halves):
            at = 2 * (x * halves + part)
            piece = pltpu.roll(columns, cz - at - 1, 1)
            out.append(jnp.where((lane == 0) | (lane == cz - 1), piece, 0.0))
        return jnp.concatenate(out, axis=0)

    def y_rows(side):
        return pl.ds(0 if side == 0 else cy - 1, chans, stride=cy)

    def node(layer, slot, x, columns):
        total = p_s[slot, x] + z_add(columns, x)
        if x == 0:
            total = total + xrx[slot, 1]
        if x == last:
            total = total + xrx[slot, 0]
        inc_s[x] = total
        for side in range(2):
            extra = yrx[slot, 1 - side, x]
            if x == 0:
                extra = extra + xyrx[slot, 2 + (1 - side)]
            if x == last:
                extra = extra + xyrx[slot, 1 - side]
            inc_s[x, y_rows(side), :] = inc_s[x, y_rows(side), :] + extra
        stacked = jnp.concatenate([h_s[x], inc_s[x].astype(BF16)], axis=0)
        half = dot(mat_n[layer], stacked) + bias_n[layer]
        step = dot(mat_no[layer], silu_of_half(half).astype(BF16))
        return (h_s[x].astype(F32) + step).astype(BF16).astype(F32)

    middle = list(range(1, last))

    def middle_edges(layer, slot):
        for x in middle:
            (wz,) = edges_xz(layer, [(x, 2)])
            (wy,) = edges_y(layer, [x])
            put(slot, x, both_z(wz) + both_y(wy), False)

    turn_s[1] = jnp.zeros_like(turn_s[1])
    middle_edges(0, 0)
    greetings = -1 + functools.reduce(
        lambda a, b: a * b,
        [
            1 + (pos > 0).astype(jnp.int32) + (pos < size - 1).astype(jnp.int32)
            for pos, size in zip(place, sizes)
        ],
    )

    def layer_step(layer, carry):
        slot = layer
        w0, wz = edges_xz(layer, [(0, 0), (0, 2)])
        (wy,) = edges_y(layer, [0])
        put(slot, 0, w0 + both_z(wz) + both_y(wy), False)

        @pl.when(layer == 0)
        def _():
            pl.semaphore_wait(barrier, greetings)

        for way in x_ways:
            if way[0] < 0:
                start(way, slot)
        ring = [(x, 0) for x in range(1, cx)]
        *wx, wz = edges_xz(layer, ring + [(last, 2)])
        (wy,) = edges_y(layer, [last])
        wx = [w0] + wx
        put(slot, last, wx[last - 1] + wx[last] + both_z(wz) + both_y(wy), False)
        for way in x_ways:
            if way[0] > 0:
                start(way, slot)
        for x in middle:
            put(slot, x, wx[x - 1] + wx[x], True)
        for side in range(2):
            for x in range(cx):
                ysend[slot, side, x] = p_s[slot, x, y_rows(side), :]
        for way in y_ways:
            start(way, slot)
        z_faces(slot)
        for way in z_ways:
            start(way, slot)

        @pl.when(layer + 1 < layers)
        def _():
            build(layer + 1)

        for way in y_ways + z_ways:
            arrive(way, slot)
        columns = z_columns(slot)
        for x in middle:
            keep_nodes(x, node(layer, slot, x, columns))

        @pl.when(layer + 1 < layers)
        def _():
            middle_edges(layer + 1, layer + 1)

        for way in x_ways:
            arrive(way, slot)
        keep_nodes(0, node(layer, slot, 0, columns))
        keep_nodes(last, node(layer, slot, last, columns))
        return carry

    def sent_step(layer, carry):
        for way in ways:
            sent(way, layer)
        return carry

    lax.fori_loop(0, layers, layer_step, 0)
    lax.fori_loop(0, layers, sent_step, 0)
    for x in range(cx):
        out_ref[:, x] = h_s[x].astype(F32).reshape(chans, cy, cz).astype(BF16)


def solution(mesh):
    sizes = tuple(mesh.shape[axis] for axis in AXES)

    def on_device(features, edge_state, multiplicity, *params):
        layers = params[0].shape[0]
        chans, cx, cy, cz = features.shape
        rows = chans * cy
        assert cz == 128 and rows % 128 == 0 and cy % 8 == 0 and cx > 1
        slots = layers
        ways = len(ways_of(sizes))
        zrows = -(-cx * (rows // 128) // 8) * 8
        vmem = pl.BlockSpec(memory_space=pltpu.VMEM)
        scratch = [pltpu.VMEM(a.shape, a.dtype) for a in (features, edge_state, multiplicity, *params)]
        scratch += [
            pltpu.VMEM((cx, rows, cz), BF16),
            pltpu.VMEM((cx, rows, cz), BF16),
            pltpu.VMEM((3, cx, rows, cz), BF16),
            pltpu.VMEM((3, cx, cy, cz), F32),
            pltpu.VMEM((slots, cx, rows, cz), F32),
            pltpu.VMEM((cx, rows, cz), F32),
            pltpu.VMEM((layers, rows, 4 * rows), BF16),
            pltpu.VMEM((layers, rows, rows), BF16),
            pltpu.VMEM((layers, rows, 2 * rows), BF16),
            pltpu.VMEM((layers, rows, rows), BF16),
            pltpu.VMEM((layers, rows, cz), F32),
            pltpu.VMEM((layers, rows, cz), F32),
            pltpu.VMEM((slots, 2, cx, chans, cz), F32),
            pltpu.VMEM((slots, 2, zrows, 128), F32),
            pltpu.VMEM((slots, 2, rows, cz), F32),
            pltpu.VMEM((slots, 2, cx, chans, cz), F32),
            pltpu.VMEM((slots, 4, chans, cz), F32),
            pltpu.VMEM((slots, 2, 9, zrows, 128), F32),
            pltpu.VMEM((2, 128, 128), F32),
            pltpu.SemaphoreType.DMA((9,)),
            pltpu.SemaphoreType.DMA((slots, ways)),
            pltpu.SemaphoreType.DMA((slots, ways)),
        ]
        return pl.pallas_call(
            functools.partial(kernel, sizes, layers),
            out_shape=jax.ShapeDtypeStruct(features.shape, features.dtype),
            in_specs=[pl.BlockSpec(memory_space=pltpu.HBM)] * 9,
            out_specs=vmem,
            scratch_shapes=scratch,
            compiler_params=pltpu.CompilerParams(
                collective_id=0, has_side_effects=True, vmem_limit_bytes=60 * 1024 * 1024
            ),
        )(features, edge_state, multiplicity, *params)

    placed = (P(None, *AXES), P(None, None, *AXES), P(*AXES)) + (P(),) * 6
    return jax.shard_map(
        on_device, mesh=mesh, in_specs=placed, out_specs=P(None, *AXES), check_vma=False
    )
```

```python
import functools
import itertools

import jax
import jax.numpy as jnp
from jax import lax
from jax.experimental import pallas as pl
from jax.experimental.pallas import tpu as pltpu
from jax.sharding import PartitionSpec as P

MESH = pl.DeviceIdType.MESH
AXES = ("gx", "gy", "gz")
F32, BF16 = jnp.float32, jnp.bfloat16
STEPS = (-1, 0, 1)
FAST, SLOW = 0, 1
OTHER = 2


def iota(shape, dim):
    return lax.broadcasted_iota(jnp.int32, shape, dim)


def dot(a, b):
    return jnp.dot(a, b, preferred_element_type=F32)


def silu_of_half(half):
    return half + half * jnp.tanh(half)


def ways_of(sizes):
    z_steps = {1: (0,), 2: (0, OTHER)}.get(sizes[2], STEPS)
    ways = itertools.product(STEPS, STEPS, z_steps)
    return [
        way for way in ways if any(way) and all(s == 0 or n > 1 for s, n in zip(way, sizes))
    ]


def messages_of(sizes, cx):
    out = []
    for way in ways_of(sizes):
        dx, dy, dz = way
        tags = (None,)
        if dx == 0:
            tags = (FAST, SLOW) if dz != 0 else range(cx)
        out += [(way, tag) for tag in tags]
    return out


def kernel(
    sizes,
    layers,
    feat_hbm, edge_hbm, mult_hbm, win_hbm, wout_hbm, bin_hbm, nin_hbm, nout_hbm, bnode_hbm,
    out_ref,
    feat_ref, edge_ref, mult_ref, win_ref, wout_ref, bin_ref, nin_ref, nout_ref, bnode_ref,
    h_s, hz_s, e_s, w_s, p_s, inc_s, mat_e, mat_o, mat_n, mat_no, bias_e, bias_n,
    ysend, zsend, xrx, yrx, xyrx, zrx, turn_s, in_sem, send_sem, recv_sem,
):
    loads = [
        pltpu.make_async_copy(source, target, in_sem.at[index])
        for index, (source, target) in enumerate([
            (win_hbm, win_ref), (wout_hbm, wout_ref), (bin_hbm, bin_ref), (nin_hbm, nin_ref),
            (nout_hbm, nout_ref), (bnode_hbm, bnode_ref), (mult_hbm, mult_ref),
            (feat_hbm, feat_ref), (edge_hbm, edge_ref),
        ])
    ]
    for load in loads:
        load.start()

    chans, cx, cy, cz = feat_ref.shape
    rows = chans * cy
    halves = rows // 128
    last = cx - 1
    zrows = zsend.shape[3]
    place = [lax.axis_index(axis) for axis in AXES]

    def exists(way):
        there = None
        for pos, step, size in zip(place, way, sizes):
            if step == 0 or step == OTHER:
                continue
            here = pos > 0 if step < 0 else pos < size - 1
            there = here if there is None else there & here
        return there

    def device(way):
        return {
            axis: 1 - pos if step == OTHER else pos + step
            for axis, pos, step in zip(AXES, place, way)
        }

    def back(way):
        return tuple(step if step == OTHER else -step for step in way)

    def when_exists(way, act):
        there = exists(way)
        if there is None:
            act()
        else:
            pl.when(there)(act)

    ways = ways_of(sizes)
    messages = messages_of(sizes, cx)
    z_steps = [way[2] for way in ways if way[0] == 0 and way[1] == 0 and way[2] != 0]

    xrx[...] = jnp.zeros_like(xrx)
    yrx[...] = jnp.zeros_like(yrx)
    xyrx[...] = jnp.zeros_like(xyrx)
    zrx[...] = jnp.zeros_like(zrx)

    barrier = pltpu.get_barrier_semaphore()
    for way in ways:
        def greet(way=way):
            pl.semaphore_signal(barrier, inc=1, device_id=device(way), device_id_type=MESH)

        when_exists(way, greet)

    mine = iota((rows, chans), 0) // cy == iota((rows, chans), 1)
    spread = mine.astype(F32).astype(BF16)
    row_y, col_y = iota((cy, rows), 0), iota((cy, rows), 1) % cy
    same_y = (row_y == col_y).astype(F32)
    half_same, half_next = 0.5 * same_y, 0.5 * (row_y + 1 == col_y).astype(F32)
    col_c = iota((1, rows), 1) // cy

    def widen(weights):
        width = weights.shape[1]
        parts = []
        for part in range(width // chans):
            pick = iota((width, rows), 0) == part * chans + col_c
            parts.append(dot(weights, pick.astype(F32).astype(BF16)).astype(BF16))
        return parts

    def build(layer):
        wide = widen(win_ref[layer]) + widen(wout_ref[layer])
        wide += widen(nin_ref[layer]) + widen(nout_ref[layer])

        def block(index):
            return dot(spread, wide[index]).reshape(chans, cy, rows)

        def flat(values):
            return values.reshape(rows, rows).astype(BF16)

        own, other = block(0), block(1)
        own_same = own * half_same[None]
        mat_e[layer, :, 0:rows] = flat(own_same)
        mat_e[layer, :, rows : 2 * rows] = flat(other * half_same[None])
        mat_e[layer, :, 2 * rows : 3 * rows] = flat(block(2) * half_same[None])
        mat_e[layer, :, 3 * rows :] = flat(own_same + other * half_next[None])
        mat_o[layer] = flat(block(3) * same_y[None])
        mat_n[layer, :, 0:rows] = flat(block(4) * half_same[None])
        mat_n[layer, :, rows:] = flat(block(5) * half_same[None])
        mat_no[layer] = flat(block(6) * same_y[None])
        for source, target in ((bin_ref, bias_e), (bnode_ref, bias_n)):
            column = jnp.sum(
                jnp.where(mine, source[pl.ds(layer, 1), :], 0.0), axis=1, keepdims=True
            )
            target[layer] = jnp.broadcast_to(0.5 * column, (rows, cz))

    for load in loads[:6]:
        load.wait()
    build(0)
    for load in loads[6:]:
        load.wait()

    fluid = mult_ref[1, 1:2, 1:2] > 0
    zeros = jnp.zeros((cy, cz), jnp.int32)
    for x in range(cx):
        count = mult_ref[x]
        ahead = (
            mult_ref[x + 1] if x < last else zeros,
            jnp.where(iota((cy, cz), 0) < cy - 1, pltpu.roll(count, cy - 1, 0), 0),
            jnp.where(iota((cy, cz), 1) < cz - 1, pltpu.roll(count, cz - 1, 1), 0),
        )
        for d in range(3):
            shared = jnp.minimum(count, ahead[d])
            w_s[d, x] = jnp.where(
                fluid & (shared > 0), 1.0 / jnp.maximum(shared, 1).astype(F32), 0.0
            )

    before_end = iota((rows, cz), 1) < cz - 1

    def keep_nodes(x, values):
        h_s[x] = values.astype(BF16)
        hz_s[x] = jnp.where(before_end, pltpu.roll(values, cz - 1, 1), 0.0).astype(BF16)

    for x in range(cx):
        keep_nodes(x, feat_ref[:, x].astype(F32).reshape(rows, cz))
        for d in range(3):
            e_s[d, x] = edge_ref[d, :, x].astype(F32).reshape(rows, cz).astype(BF16)

    def finish(layer, slabs, half):
        count = len(slabs)
        half = half + jnp.concatenate([bias_e[layer]] * count, axis=1)
        message = dot(mat_o[layer], silu_of_half(half).astype(BF16))
        weighted = []
        for index, (x, d) in enumerate(slabs):
            own = message[:, index * cz : (index + 1) * cz]
            e_s[d, x] = (e_s[d, x].astype(F32) + own).astype(BF16)
            weighted.append(w_s[d, x][None] * own.reshape(chans, cy, cz))
        return weighted

    def edges_xz(layer, slabs):
        nothing = jnp.zeros((rows, cz), BF16)
        own = jnp.concatenate([h_s[x] for x, d in slabs], axis=1)
        other = jnp.concatenate(
            [hz_s[x] if d == 2 else h_s[x + 1] if x < last else nothing for x, d in slabs], axis=1
        )
        edge = jnp.concatenate([e_s[d, x] for x, d in slabs], axis=1)
        stacked = jnp.concatenate([own, other, edge], axis=0)
        return finish(layer, slabs, dot(mat_e[layer, :, 0 : 3 * rows], stacked))

    def edges_y(layer, xs):
        edge = jnp.concatenate([e_s[1, x] for x in xs], axis=1)
        own = jnp.concatenate([h_s[x] for x in xs], axis=1)
        stacked = jnp.concatenate([edge, own], axis=0)
        slabs = [(x, 1) for x in xs]
        return finish(layer, slabs, dot(mat_e[layer, :, 2 * rows :], stacked))

    def both_y(weighted):
        return weighted + pltpu.roll(weighted, 1, 1)

    def both_z(weighted):
        return weighted + pltpu.roll(weighted, 1, 2)

    def put(slot, x, value, add):
        value = value.reshape(rows, cz)
        if add:
            value = p_s[slot, x] + value
        p_s[slot, x] = value

    def transfer(message, slot, slow):
        way, tag = message
        dx, dy, dz = way
        index = messages.index(message)
        side = 0 if dy < 0 else 1
        face = 0 if dx < 0 else last
        if dz != 0:
            which = z_steps.index(dz)
            source = zsend.at[slot, which, SLOW if tag is None and face == slow else tag or FAST]
            target = zrx.at[slot, which, {-1: 0, 0: 1 + (tag or 0), 1: 3}[dx], dy + 1]
        elif dy == 0:
            source = p_s.at[slot, face]
            target = xrx.at[slot, 0 if dx < 0 else 1]
        elif dx == 0:
            source = ysend.at[slot, side, tag]
            target = yrx.at[slot, side, tag]
        else:
            source = ysend.at[slot, side, face]
            target = xyrx.at[slot, (0 if dx < 0 else 2) + side]
        return pltpu.make_async_remote_copy(
            src_ref=source,
            dst_ref=target,
            send_sem=send_sem.at[slot, index],
            recv_sem=recv_sem.at[slot, index],
            device_id=device(way),
            device_id_type=MESH,
        )

    def start(message, slot, slow):
        when_exists(message[0], lambda: transfer(message, slot, slow).start())

    def arrive(message, slot, slow):
        when_exists(back(message[0]), lambda: transfer(message, slot, slow).wait_recv())

    def sent(message, slot, slow):
        when_exists(message[0], lambda: transfer(message, slot, slow).wait_send())

    lane = iota((128, cz), 1)
    odd_rows, even_rows = pl.ds(1, zrows, stride=2), pl.ds(0, zrows, stride=2)

    def z_faces(slot, xs, phase):
        faces = jnp.zeros((128, cz), F32)
        for x in xs:
            for part in range(halves):
                at = 2 * (x * halves + part)
                piece = pltpu.roll(p_s[slot, x, part * 128 : (part + 1) * 128], at + 1, 1)
                faces = jnp.where((lane == at) | (lane == at + 1), piece, faces)
        turn_s[2] = faces.T
        first, final = turn_s[2, odd_rows, :], turn_s[2, even_rows, :]
        for which, dz in enumerate(z_steps):
            if dz == OTHER:
                zsend[slot, which, phase] = jnp.where(place[2] == 0, final, first)
            else:
                zsend[slot, which, phase] = first if dz < 0 else final

    row_z, lane_z = iota((zrows, 128), 0), iota((zrows, 128), 1)

    def z_total(slot, which, face, phase):
        total = jnp.zeros((zrows, 128), F32)
        shift_x, shift_y = last * halves, cy - 1
        for dy in STEPS:
            part = zrx[slot, which, 1 + phase, dy + 1]
            if face == 0:
                piece = zrx[slot, which, 3, dy + 1]
                piece = jnp.where(row_z < halves, pltpu.roll(piece, zrows - shift_x, 0), 0.0)
            else:
                piece = zrx[slot, which, 0, dy + 1]
                inside = (row_z >= shift_x) & (row_z < shift_x + halves)
                piece = jnp.where(inside, pltpu.roll(piece, shift_x, 0), 0.0)
            part = part + piece
            if dy > 0:
                part = jnp.where(lane_z % cy == 0, pltpu.roll(part, 128 - shift_y, 1), 0.0)
            if dy < 0:
                part = jnp.where(lane_z % cy == cy - 1, pltpu.roll(part, shift_y, 1), 0.0)
            total = total + part
        return total

    def z_columns(slot, face, phase):
        for which, dz in enumerate(z_steps):
            total = z_total(slot, which, face, phase)
            if dz != 1:
                turn_s[phase, even_rows, :] = jnp.where(place[2] < sizes[2] - 1, total, 0.0)
            if dz != -1:
                turn_s[phase, odd_rows, :] = jnp.where(place[2] > 0, total, 0.0)
        return turn_s[phase].T

    def z_add(columns, x):
        out = []
        for part in range(halves):
            at = 2 * (x * halves + part)
            piece = pltpu.roll(columns, cz - at - 1, 1)
            out.append(jnp.where((lane == 0) | (lane == cz - 1), piece, 0.0))
        return jnp.concatenate(out, axis=0)

    def y_rows(side):
        return pl.ds(0 if side == 0 else cy - 1, chans, stride=cy)

    def node(layer, slot, x, columns):
        total = p_s[slot, x] + z_add(columns, x)
        if x == 0:
            total = total + xrx[slot, 1]
        if x == last:
            total = total + xrx[slot, 0]
        inc_s[x] = total
        for side in range(2):
            extra = yrx[slot, 1 - side, x]
            if x == 0:
                extra = extra + xyrx[slot, 2 + (1 - side)]
            if x == last:
                extra = extra + xyrx[slot, 1 - side]
            inc_s[x, y_rows(side), :] = inc_s[x, y_rows(side), :] + extra
        stacked = jnp.concatenate([h_s[x], inc_s[x].astype(BF16)], axis=0)
        half = dot(mat_n[layer], stacked) + bias_n[layer]
        step = dot(mat_no[layer], silu_of_half(half).astype(BF16))
        return (h_s[x].astype(F32) + step).astype(BF16).astype(F32)

    turn_s[...] = jnp.zeros_like(turn_s)
    greetings = -1 + functools.reduce(
        lambda a, b: a * b,
        [
            1 + (pos > 0).astype(jnp.int32) + (pos < size - 1).astype(jnp.int32)
            for pos, size in zip(place, sizes)
        ],
    )
    middle = list(range(1, last))

    def run(slow):
        fast = last - slow

        def phase_of(message, sending):
            (dx, dy, dz), tag = message
            if dx != 0:
                face = 0 if (dx < 0) == sending else last
                return FAST if face == fast else SLOW
            if dz != 0:
                return tag
            return FAST if tag == fast else SLOW

        def order(message):
            (dx, dy, dz), tag = message
            return (dy != 0 or dz != 0, dz != 0)

        ordered = sorted(messages, key=order)

        def starts(slot, phase, first):
            for message in ordered:
                if phase_of(message, True) == phase and (order(message) == (False, False)) == first:
                    start(message, slot, slow)

        def arrivals(slot, phase, pick):
            for message in ordered:
                if phase_of(message, False) == phase and pick(message):
                    arrive(message, slot, slow)

        def face_group(face):
            edge = 0 if face == 0 else last - 1
            absent = [(last, 0)] if face == last else []
            return [(edge, 0)] + absent + [(face, 2)]

        def put_face(slot, face, weighted, wy):
            shared, *absent, wz = weighted
            total = shared + both_z(wz) + both_y(wy)
            for extra in absent:
                total = total + extra
            put(slot, face, total, False)
            put(slot, 1 if face == 0 else last - 1, shared, True)

        def stage_y(slot, xs):
            for side in range(2):
                for x in xs:
                    ysend[slot, side, x] = p_s[slot, x, y_rows(side), :]

        def ahead_edges(layer):
            inner = [(x, 0) for x in middle[:-1]]
            group = [(x, 2) for x in middle] + inner
            weighted = edges_xz(layer, group + face_group(fast))
            wy = edges_y(layer, middle + [fast])
            for index, x in enumerate(middle):
                put(layer, x, both_z(weighted[index]) + both_y(wy[index]), False)
            for index, (x, d) in enumerate(inner):
                put(layer, x, weighted[len(middle) + index], True)
                put(layer, x + 1, weighted[len(middle) + index], True)
            put_face(layer, fast, weighted[len(group) :], wy[-1])

        def fast_sends(slot):
            starts(slot, FAST, True)
            stage_y(slot, [fast])
            z_faces(slot, [fast], FAST)
            starts(slot, FAST, False)

        ahead_edges(0)
        pl.semaphore_wait(barrier, greetings)
        fast_sends(0)

        def layer_step(layer, carry):
            slot = layer
            weighted = edges_xz(layer, face_group(slow))
            (wy,) = edges_y(layer, [slow])
            put_face(slot, slow, weighted, wy)
            starts(slot, SLOW, True)
            stage_y(slot, [slow] + middle)
            z_faces(slot, [slow] + middle, SLOW)
            starts(slot, SLOW, False)

            @pl.when(layer + 1 < layers)
            def _():
                build(layer + 1)

            arrivals(slot, FAST, lambda message: True)
            columns = z_columns(slot, fast, FAST)
            keep_nodes(fast, node(layer, slot, fast, columns))

            def late(message):
                (dx, dy, dz), tag = message
                return dz == 0 and (dx != 0 or tag == slow)

            arrivals(slot, SLOW, lambda message: not late(message))
            columns = z_columns(slot, slow, SLOW)
            for x in middle:
                keep_nodes(x, node(layer, slot, x, columns))

            @pl.when(layer + 1 < layers)
            def _():
                ahead_edges(layer + 1)
                fast_sends(layer + 1)

            arrivals(slot, SLOW, late)
            keep_nodes(slow, node(layer, slot, slow, columns))
            return carry

        def sent_step(layer, carry):
            for message in messages:
                sent(message, layer, slow)
            return carry

        lax.fori_loop(0, layers, layer_step, 0)
        lax.fori_loop(0, layers, sent_step, 0)

    pl.when(lax.rem(place[0], 2) == 0)(lambda: run(0))
    pl.when(lax.rem(place[0], 2) == 1)(lambda: run(last))
    for x in range(cx):
        out_ref[:, x] = h_s[x].astype(F32).reshape(chans, cy, cz)


def solution(mesh):
    sizes = tuple(mesh.shape[axis] for axis in AXES)

    def on_device(features, edge_state, multiplicity, *params):
        layers = params[0].shape[0]
        chans, cx, cy, cz = features.shape
        rows = chans * cy
        assert cz == 128 and rows % 128 == 0 and cy % 8 == 0 and cx > 2
        slots = layers
        ways = len(messages_of(sizes, cx))
        zrows = -(-cx * (rows // 128) // 8) * 8
        vmem = pl.BlockSpec(memory_space=pltpu.VMEM)
        scratch = [pltpu.VMEM(a.shape, a.dtype) for a in (features, edge_state, multiplicity, *params)]
        scratch += [
            pltpu.VMEM((cx, rows, cz), BF16),
            pltpu.VMEM((cx, rows, cz), BF16),
            pltpu.VMEM((3, cx, rows, cz), BF16),
            pltpu.VMEM((3, cx, cy, cz), F32),
            pltpu.VMEM((slots, cx, rows, cz), F32),
            pltpu.VMEM((cx, rows, cz), F32),
            pltpu.VMEM((layers, rows, 4 * rows), BF16),
            pltpu.VMEM((layers, rows, rows), BF16),
            pltpu.VMEM((layers, rows, 2 * rows), BF16),
            pltpu.VMEM((layers, rows, rows), BF16),
            pltpu.VMEM((layers, rows, cz), F32),
            pltpu.VMEM((layers, rows, cz), F32),
            pltpu.VMEM((slots, 2, cx, chans, cz), F32),
            pltpu.VMEM((slots, 2, 2, zrows, 128), F32),
            pltpu.VMEM((slots, 2, rows, cz), F32),
            pltpu.VMEM((slots, 2, cx, chans, cz), F32),
            pltpu.VMEM((slots, 4, chans, cz), F32),
            pltpu.VMEM((slots, 2, 4, 3, zrows, 128), F32),
            pltpu.VMEM((3, 128, 128), F32),
            pltpu.SemaphoreType.DMA((9,)),
            pltpu.SemaphoreType.DMA((slots, ways)),
            pltpu.SemaphoreType.DMA((slots, ways)),
        ]
        nodes = pl.pallas_call(
            functools.partial(kernel, sizes, layers),
            out_shape=jax.ShapeDtypeStruct(features.shape, F32),
            in_specs=[pl.BlockSpec(memory_space=pltpu.HBM)] * 9,
            out_specs=vmem,
            scratch_shapes=scratch,
            compiler_params=pltpu.CompilerParams(
                collective_id=0, has_side_effects=True, vmem_limit_bytes=60 * 1024 * 1024
            ),
        )(features, edge_state, multiplicity, *params)
        return nodes.astype(features.dtype)

    placed = (P(None, *AXES), P(None, None, *AXES), P(*AXES)) + (P(),) * 6
    return jax.shard_map(
        on_device, mesh=mesh, in_specs=placed, out_specs=P(None, *AXES), check_vma=False
    )
```

```python
import functools
import itertools

import jax
import jax.numpy as jnp
from jax import lax
from jax.experimental import pallas as pl
from jax.experimental.pallas import tpu as pltpu
from jax.sharding import PartitionSpec as P

MESH = pl.DeviceIdType.MESH
AXES = ("gx", "gy", "gz")
F32, BF16 = jnp.float32, jnp.bfloat16
STEPS = (-1, 0, 1)
FAST, SLOW = 0, 1
OTHER = 2


def iota(shape, dim):
    return lax.broadcasted_iota(jnp.int32, shape, dim)


def dot(a, b):
    return jnp.dot(a, b, preferred_element_type=F32)


def silu_of_half(half):
    return half + half * jnp.tanh(half)


def ways_of(sizes):
    z_steps = {1: (0,), 2: (0, OTHER)}.get(sizes[2], STEPS)
    ways = itertools.product(STEPS, STEPS, z_steps)
    return [
        way for way in ways if any(way) and all(s == 0 or n > 1 for s, n in zip(way, sizes))
    ]


def messages_of(sizes):
    out = []
    for way in ways_of(sizes):
        dx, dy, dz = way
        out += [(way, tag) for tag in ((FAST, SLOW) if dx == 0 else (None,))]
    return out


def kernel(
    sizes,
    layers,
    feat_hbm, edge_hbm, mult_hbm, win_hbm, wout_hbm, bin_hbm, nin_hbm, nout_hbm, bnode_hbm,
    out_ref,
    feat_ref, edge_ref, mult_ref, win_ref, wout_ref, bin_ref, nin_ref, nout_ref, bnode_ref,
    h_s, hz_s, e_s, w_s, p_s, inc_s, mat_e, mat_o, mat_n, mat_no, bias_e, bias_n,
    ysend, zsend, xrx, yrx, xyrx, zrx, turn_s, in_sem, send_sem, recv_sem,
):
    loads = [
        pltpu.make_async_copy(source, target, in_sem.at[index])
        for index, (source, target) in enumerate([
            (win_hbm, win_ref), (wout_hbm, wout_ref), (bin_hbm, bin_ref), (nin_hbm, nin_ref),
            (nout_hbm, nout_ref), (bnode_hbm, bnode_ref), (mult_hbm, mult_ref),
            (feat_hbm, feat_ref), (edge_hbm, edge_ref),
        ])
    ]
    for load in loads:
        load.start()

    chans, cx, cy, cz = feat_ref.shape
    rows = chans * cy
    halves = rows // 128
    last = cx - 1
    zrows = zsend.shape[3]
    place = [lax.axis_index(axis) for axis in AXES]

    def exists(way):
        there = None
        for pos, step, size in zip(place, way, sizes):
            if step == 0 or step == OTHER:
                continue
            here = pos > 0 if step < 0 else pos < size - 1
            there = here if there is None else there & here
        return there

    def device(way):
        return {
            axis: 1 - pos if step == OTHER else pos + step
            for axis, pos, step in zip(AXES, place, way)
        }

    def back(way):
        return tuple(step if step == OTHER else -step for step in way)

    def when_exists(way, act):
        there = exists(way)
        if there is None:
            act()
        else:
            pl.when(there)(act)

    ways = ways_of(sizes)
    messages = messages_of(sizes)
    z_steps = [way[2] for way in ways if way[0] == 0 and way[1] == 0 and way[2] != 0]

    xrx[...] = jnp.zeros_like(xrx)
    yrx[...] = jnp.zeros_like(yrx)
    xyrx[...] = jnp.zeros_like(xyrx)
    zrx[...] = jnp.zeros_like(zrx)

    barrier = pltpu.get_barrier_semaphore()
    for way in ways:
        def greet(way=way):
            pl.semaphore_signal(barrier, inc=1, device_id=device(way), device_id_type=MESH)

        when_exists(way, greet)

    mine = iota((rows, chans), 0) // cy == iota((rows, chans), 1)
    spread = mine.astype(F32).astype(BF16)
    row_y, col_y = iota((cy, rows), 0), iota((cy, rows), 1) % cy
    same_y = (row_y == col_y).astype(F32)
    half_same, half_next = 0.5 * same_y, 0.5 * (row_y + 1 == col_y).astype(F32)
    col_c = iota((1, rows), 1) // cy

    def widen(weights):
        width = weights.shape[1]
        parts = []
        for part in range(width // chans):
            pick = iota((width, rows), 0) == part * chans + col_c
            parts.append(dot(weights, pick.astype(F32).astype(BF16)).astype(BF16))
        return parts

    def build(layer):
        wide = widen(win_ref[layer]) + widen(wout_ref[layer])
        wide += widen(nin_ref[layer]) + widen(nout_ref[layer])

        def block(index):
            return dot(spread, wide[index]).reshape(chans, cy, rows)

        def flat(values):
            return values.reshape(rows, rows).astype(BF16)

        own, other = block(0), block(1)
        own_same = own * half_same[None]
        mat_e[layer, :, 0:rows] = flat(own_same)
        mat_e[layer, :, rows : 2 * rows] = flat(other * half_same[None])
        mat_e[layer, :, 2 * rows : 3 * rows] = flat(block(2) * half_same[None])
        mat_e[layer, :, 3 * rows :] = flat(own_same + other * half_next[None])
        mat_o[layer] = flat(block(3) * same_y[None])
        mat_n[layer, :, 0:rows] = flat(block(4) * half_same[None])
        mat_n[layer, :, rows:] = flat(block(5) * half_same[None])
        mat_no[layer] = flat(block(6) * same_y[None])
        for source, target in ((bin_ref, bias_e), (bnode_ref, bias_n)):
            column = jnp.sum(
                jnp.where(mine, source[pl.ds(layer, 1), :], 0.0), axis=1, keepdims=True
            )
            target[layer] = jnp.broadcast_to(0.5 * column, (rows, cz))

    for load in loads[:6]:
        load.wait()
    build(0)
    for load in loads[6:]:
        load.wait()

    fluid = mult_ref[1, 1:2, 1:2] > 0
    zeros = jnp.zeros((cy, cz), jnp.int32)
    for x in range(cx):
        count = mult_ref[x]
        ahead = (
            mult_ref[x + 1] if x < last else zeros,
            jnp.where(iota((cy, cz), 0) < cy - 1, pltpu.roll(count, cy - 1, 0), 0),
            jnp.where(iota((cy, cz), 1) < cz - 1, pltpu.roll(count, cz - 1, 1), 0),
        )
        for d in range(3):
            shared = jnp.minimum(count, ahead[d])
            w_s[d, x] = jnp.where(
                fluid & (shared > 0), 1.0 / jnp.maximum(shared, 1).astype(F32), 0.0
            )

    before_end = iota((rows, cz), 1) < cz - 1

    def keep_nodes(x, values):
        h_s[x] = values.astype(BF16)
        hz_s[x] = jnp.where(before_end, pltpu.roll(values, cz - 1, 1), 0.0).astype(BF16)

    for x in range(cx):
        keep_nodes(x, feat_ref[:, x].astype(F32).reshape(rows, cz))
        for d in range(3):
            e_s[d, x] = edge_ref[d, :, x].astype(F32).reshape(rows, cz).astype(BF16)

    def finish(layer, slabs, half):
        count = len(slabs)
        half = half + jnp.concatenate([bias_e[layer]] * count, axis=1)
        message = dot(mat_o[layer], silu_of_half(half).astype(BF16))
        weighted = []
        for index, (x, d) in enumerate(slabs):
            own = message[:, index * cz : (index + 1) * cz]
            e_s[d, x] = (e_s[d, x].astype(F32) + own).astype(BF16)
            weighted.append(w_s[d, x][None] * own.reshape(chans, cy, cz))
        return weighted

    def edges_xz(layer, slabs):
        nothing = jnp.zeros((rows, cz), BF16)
        own = jnp.concatenate([h_s[x] for x, d in slabs], axis=1)
        other = jnp.concatenate(
            [hz_s[x] if d == 2 else h_s[x + 1] if x < last else nothing for x, d in slabs], axis=1
        )
        edge = jnp.concatenate([e_s[d, x] for x, d in slabs], axis=1)
        stacked = jnp.concatenate([own, other, edge], axis=0)
        return finish(layer, slabs, dot(mat_e[layer, :, 0 : 3 * rows], stacked))

    def edges_y(layer, xs):
        edge = jnp.concatenate([e_s[1, x] for x in xs], axis=1)
        own = jnp.concatenate([h_s[x] for x in xs], axis=1)
        stacked = jnp.concatenate([edge, own], axis=0)
        slabs = [(x, 1) for x in xs]
        return finish(layer, slabs, dot(mat_e[layer, :, 2 * rows :], stacked))

    def both_y(weighted):
        return weighted + pltpu.roll(weighted, 1, 1)

    def both_z(weighted):
        return weighted + pltpu.roll(weighted, 1, 2)

    def put(slot, x, value, add):
        value = value.reshape(rows, cz)
        if add:
            value = p_s[slot, x] + value
        p_s[slot, x] = value

    def transfer(message, slot, slow):
        way, tag = message
        dx, dy, dz = way
        index = messages.index(message)
        side = 0 if dy < 0 else 1
        face = 0 if dx < 0 else last
        if dz != 0:
            which = z_steps.index(dz)
            source = zsend.at[slot, which, SLOW if tag is None and face == slow else tag or FAST]
            target = zrx.at[slot, which, {-1: 0, 0: 1 + (tag or 0), 1: 3}[dx], dy + 1]
        elif dy == 0:
            source = p_s.at[slot, face]
            target = xrx.at[slot, 0 if dx < 0 else 1]
        elif dx == 0:
            slabs = pl.ds(last - slow, 1) if tag == FAST else pl.ds(0 if slow == 0 else 1, last)
            source = ysend.at[slot, side, slabs]
            target = yrx.at[slot, side, slabs]
        else:
            source = ysend.at[slot, side, face]
            target = xyrx.at[slot, (0 if dx < 0 else 2) + side]
        return pltpu.make_async_remote_copy(
            src_ref=source,
            dst_ref=target,
            send_sem=send_sem.at[slot, index],
            recv_sem=recv_sem.at[slot, index],
            device_id=device(way),
            device_id_type=MESH,
        )

    def start(message, slot, slow):
        when_exists(message[0], lambda: transfer(message, slot, slow).start())

    def arrive(message, slot, slow):
        when_exists(back(message[0]), lambda: transfer(message, slot, slow).wait_recv())

    def sent(message, slot, slow):
        when_exists(message[0], lambda: transfer(message, slot, slow).wait_send())

    lane = iota((128, cz), 1)
    odd_rows, even_rows = pl.ds(1, zrows, stride=2), pl.ds(0, zrows, stride=2)

    def z_faces(slot, xs, phase):
        faces = jnp.zeros((128, cz), F32)
        for x in xs:
            for part in range(halves):
                at = 2 * (x * halves + part)
                piece = pltpu.roll(p_s[slot, x, part * 128 : (part + 1) * 128], at + 1, 1)
                faces = jnp.where((lane == at) | (lane == at + 1), piece, faces)
        turn_s[2] = faces.T
        first, final = turn_s[2, odd_rows, :], turn_s[2, even_rows, :]
        for which, dz in enumerate(z_steps):
            if dz == OTHER:
                zsend[slot, which, phase] = jnp.where(place[2] == 0, final, first)
            else:
                zsend[slot, which, phase] = first if dz < 0 else final

    row_z, lane_z = iota((zrows, 128), 0), iota((zrows, 128), 1)

    def z_total(slot, which, face, phase):
        total = jnp.zeros((zrows, 128), F32)
        shift_x, shift_y = last * halves, cy - 1
        for dy in STEPS:
            part = zrx[slot, which, 1 + phase, dy + 1]
            if face == 0:
                piece = zrx[slot, which, 3, dy + 1]
                piece = jnp.where(row_z < halves, pltpu.roll(piece, zrows - shift_x, 0), 0.0)
            else:
                piece = zrx[slot, which, 0, dy + 1]
                inside = (row_z >= shift_x) & (row_z < shift_x + halves)
                piece = jnp.where(inside, pltpu.roll(piece, shift_x, 0), 0.0)
            part = part + piece
            if dy > 0:
                part = jnp.where(lane_z % cy == 0, pltpu.roll(part, 128 - shift_y, 1), 0.0)
            if dy < 0:
                part = jnp.where(lane_z % cy == cy - 1, pltpu.roll(part, shift_y, 1), 0.0)
            total = total + part
        return total

    def z_columns(slot, face, phase):
        for which, dz in enumerate(z_steps):
            total = z_total(slot, which, face, phase)
            if dz != 1:
                turn_s[phase, even_rows, :] = jnp.where(place[2] < sizes[2] - 1, total, 0.0)
            if dz != -1:
                turn_s[phase, odd_rows, :] = jnp.where(place[2] > 0, total, 0.0)
        return turn_s[phase].T

    def z_add(columns, x):
        out = []
        for part in range(halves):
            at = 2 * (x * halves + part)
            piece = pltpu.roll(columns, cz - at - 1, 1)
            out.append(jnp.where((lane == 0) | (lane == cz - 1), piece, 0.0))
        return jnp.concatenate(out, axis=0)

    def y_rows(side):
        return pl.ds(0 if side == 0 else cy - 1, chans, stride=cy)

    def node(layer, slot, x, columns):
        total = p_s[slot, x] + z_add(columns, x)
        if x == 0:
            total = total + xrx[slot, 1]
        if x == last:
            total = total + xrx[slot, 0]
        inc_s[x] = total
        for side in range(2):
            extra = yrx[slot, 1 - side, x]
            if x == 0:
                extra = extra + xyrx[slot, 2 + (1 - side)]
            if x == last:
                extra = extra + xyrx[slot, 1 - side]
            inc_s[x, y_rows(side), :] = inc_s[x, y_rows(side), :] + extra
        stacked = jnp.concatenate([h_s[x], inc_s[x].astype(BF16)], axis=0)
        half = dot(mat_n[layer], stacked) + bias_n[layer]
        step = dot(mat_no[layer], silu_of_half(half).astype(BF16))
        return (h_s[x].astype(F32) + step).astype(BF16).astype(F32)

    turn_s[...] = jnp.zeros_like(turn_s)
    greetings = -1 + functools.reduce(
        lambda a, b: a * b,
        [
            1 + (pos > 0).astype(jnp.int32) + (pos < size - 1).astype(jnp.int32)
            for pos, size in zip(place, sizes)
        ],
    )
    middle = list(range(1, last))

    def run(slow):
        fast = last - slow

        def phase_of(message, sending):
            (dx, dy, dz), tag = message
            if dx != 0:
                face = 0 if (dx < 0) == sending else last
                return FAST if face == fast else SLOW
            return tag

        def order(message):
            (dx, dy, dz), tag = message
            return (dy != 0 or dz != 0, dz != 0)

        ordered = sorted(messages, key=order)

        def starts(slot, phase, first):
            for message in ordered:
                if phase_of(message, True) == phase and (order(message) == (False, False)) == first:
                    start(message, slot, slow)

        def arrivals(slot, phase, pick):
            for message in ordered:
                if phase_of(message, False) == phase and pick(message):
                    arrive(message, slot, slow)

        def shared_edge(face):
            return (0 if face == 0 else last - 1, 0)

        def own_edges(face):
            return ([(last, 0)] if face == last else []) + [(face, 2)]

        def inside(weighted, wy):
            *absent, wz = weighted
            return sum(absent, both_z(wz) + both_y(wy))

        def put_shared(slot, face, shared):
            put(slot, 1 if face == 0 else last - 1, shared, True)

        def stage_y(slot, xs):
            for side in range(2):
                for x in xs:
                    ysend[slot, side, x] = p_s[slot, x, y_rows(side), :]

        def fast_edges(layer):
            weighted = edges_xz(layer, own_edges(fast))
            (wy,) = edges_y(layer, [fast])
            put(layer, fast, inside(weighted, wy), False)

        def middle_edges(layer):
            inner = [(x, 0) for x in middle[:-1]]
            group = [(x, 2) for x in middle] + [shared_edge(fast)] + inner
            weighted = edges_xz(layer, group)
            wy = edges_y(layer, middle)
            for index, x in enumerate(middle):
                put(layer, x, both_z(weighted[index]) + both_y(wy[index]), False)
            shared, *inner_weighted = weighted[len(middle) :]
            for (x, d), value in zip(inner, inner_weighted):
                put(layer, x, value, True)
                put(layer, x + 1, value, True)
            put(layer, fast, shared, True)
            put_shared(layer, fast, shared)

        def fast_sends(slot):
            starts(slot, FAST, True)
            stage_y(slot, [fast])
            z_faces(slot, [fast], FAST)
            starts(slot, FAST, False)

        fast_edges(0)
        middle_edges(0)
        pl.semaphore_wait(barrier, greetings)
        fast_sends(0)

        def layer_step(layer, carry):
            slot = layer
            shared, *weighted = edges_xz(layer, [shared_edge(slow)] + own_edges(slow))
            (wy,) = edges_y(layer, [slow])
            put(slot, slow, shared + inside(weighted, wy), False)
            starts(slot, SLOW, True)
            put_shared(slot, slow, shared)
            stage_y(slot, [slow] + middle)
            z_faces(slot, [slow] + middle, SLOW)
            starts(slot, SLOW, False)

            @pl.when(layer + 1 < layers)
            def _():
                build(layer + 1)

            arrivals(slot, FAST, lambda message: True)
            columns = z_columns(slot, fast, FAST)
            keep_nodes(fast, node(layer, slot, fast, columns))

            @pl.when(layer + 1 < layers)
            def _():
                fast_edges(layer + 1)

            def late(message):
                (dx, dy, dz), tag = message
                return dz == 0 and dx != 0

            arrivals(slot, SLOW, lambda message: not late(message))
            columns = z_columns(slot, slow, SLOW)
            for x in middle:
                keep_nodes(x, node(layer, slot, x, columns))

            @pl.when(layer + 1 < layers)
            def _():
                middle_edges(layer + 1)
                fast_sends(layer + 1)

            for message in messages:
                sent(message, layer, slow)
            arrivals(slot, SLOW, late)
            keep_nodes(slow, node(layer, slot, slow, columns))
            return carry

        lax.fori_loop(0, layers, layer_step, 0)

    pl.when(lax.rem(place[0], 2) == 0)(lambda: run(0))
    pl.when(lax.rem(place[0], 2) == 1)(lambda: run(last))
    for x in range(cx):
        out_ref[:, x] = h_s[x].astype(F32).reshape(chans, cy, cz).astype(BF16)


def solution(mesh):
    sizes = tuple(mesh.shape[axis] for axis in AXES)

    def on_device(features, edge_state, multiplicity, *params):
        layers = params[0].shape[0]
        chans, cx, cy, cz = features.shape
        rows = chans * cy
        assert cz == 128 and rows % 128 == 0 and cy % 8 == 0 and cx > 2
        slots = layers
        ways = len(messages_of(sizes))
        zrows = -(-cx * (rows // 128) // 8) * 8
        vmem = pl.BlockSpec(memory_space=pltpu.VMEM)
        scratch = [pltpu.VMEM(a.shape, a.dtype) for a in (features, edge_state, multiplicity, *params)]
        scratch += [
            pltpu.VMEM((cx, rows, cz), BF16),
            pltpu.VMEM((cx, rows, cz), BF16),
            pltpu.VMEM((3, cx, rows, cz), BF16),
            pltpu.VMEM((3, cx, cy, cz), F32),
            pltpu.VMEM((slots, cx, rows, cz), F32),
            pltpu.VMEM((cx, rows, cz), F32),
            pltpu.VMEM((layers, rows, 4 * rows), BF16),
            pltpu.VMEM((layers, rows, rows), BF16),
            pltpu.VMEM((layers, rows, 2 * rows), BF16),
            pltpu.VMEM((layers, rows, rows), BF16),
            pltpu.VMEM((layers, rows, cz), F32),
            pltpu.VMEM((layers, rows, cz), F32),
            pltpu.VMEM((slots, 2, cx, chans, cz), F32),
            pltpu.VMEM((slots, 2, 2, zrows, 128), F32),
            pltpu.VMEM((slots, 2, rows, cz), F32),
            pltpu.VMEM((slots, 2, cx, chans, cz), F32),
            pltpu.VMEM((slots, 4, chans, cz), F32),
            pltpu.VMEM((slots, 2, 4, 3, zrows, 128), F32),
            pltpu.VMEM((3, 128, 128), F32),
            pltpu.SemaphoreType.DMA((9,)),
            pltpu.SemaphoreType.DMA((slots, ways)),
            pltpu.SemaphoreType.DMA((slots, ways)),
        ]
        return pl.pallas_call(
            functools.partial(kernel, sizes, layers),
            out_shape=pltpu.VMEM(features.shape, features.dtype),
            in_specs=[pl.BlockSpec(memory_space=pltpu.HBM)] * 9,
            out_specs=vmem,
            scratch_shapes=scratch,
            compiler_params=pltpu.CompilerParams(
                collective_id=0, has_side_effects=True, vmem_limit_bytes=60 * 1024 * 1024
            ),
        )(features, edge_state, multiplicity, *params)

    placed = (P(None, *AXES), P(None, None, *AXES), P(*AXES)) + (P(),) * 6
    return jax.shard_map(
        on_device, mesh=mesh, in_specs=placed, out_specs=P(None, *AXES), check_vma=False
    )
```

```python
import functools
import itertools

import jax
import jax.numpy as jnp
from jax import lax
from jax.experimental import pallas as pl
from jax.experimental.pallas import tpu as pltpu
from jax.sharding import PartitionSpec as P

MESH = pl.DeviceIdType.MESH
AXES = ("gx", "gy", "gz")
F32, BF16 = jnp.float32, jnp.bfloat16
STEPS = (-1, 0, 1)
FAST, SLOW = 0, 1
OTHER = 2


def iota(shape, dim):
    return lax.broadcasted_iota(jnp.int32, shape, dim)


def dot(a, b):
    return jnp.dot(a, b, preferred_element_type=F32)


def silu_of_half(half):
    return half + half * jnp.tanh(half)


def ways_of(sizes):
    z_steps = {1: (0,), 2: (0, OTHER)}.get(sizes[2], STEPS)
    ways = itertools.product(STEPS, STEPS, z_steps)
    return [
        way for way in ways if any(way) and all(s == 0 or n > 1 for s, n in zip(way, sizes))
    ]


def messages_of(sizes):
    out = []
    for way in ways_of(sizes):
        dx, dy, dz = way
        out += [(way, tag) for tag in ((FAST, SLOW) if dx == 0 else (None,))]
    return out


def kernel(
    sizes,
    layers,
    feat_hbm, edge_hbm, mult_hbm, win_hbm, wout_hbm, bin_hbm, nin_hbm, nout_hbm, bnode_hbm,
    out_ref,
    feat_ref, edge_ref, mult_ref, win_ref, wout_ref, bin_ref, nin_ref, nout_ref, bnode_ref,
    stage_s, h_s, hz_s, e_s, w_s, p_s, bias_e, bias_n,
    zsend, xrx, yrx, xyrx, zrx, turn_s, in_sem, send_sem, recv_sem,
):
    loads = [
        pltpu.make_async_copy(source, target, in_sem.at[index])
        for index, (source, target) in enumerate([
            (win_hbm, win_ref), (wout_hbm, wout_ref), (bin_hbm, bin_ref), (nin_hbm, nin_ref),
            (nout_hbm, nout_ref), (bnode_hbm, bnode_ref), (mult_hbm, mult_ref),
            (feat_hbm, feat_ref), (edge_hbm, edge_ref),
        ])
    ]
    for load in loads:
        load.start()

    chans, cx, cy, cz = feat_ref.shape
    rows, cells = chans * cy, cy * cz
    halves = rows // 128
    per_half = cy // halves
    last = cx - 1
    zrows = zsend.shape[3]
    place = [lax.axis_index(axis) for axis in AXES]

    def exists(way):
        there = None
        for pos, step, size in zip(place, way, sizes):
            if step == 0 or step == OTHER:
                continue
            here = pos > 0 if step < 0 else pos < size - 1
            there = here if there is None else there & here
        return there

    def device(way):
        return {
            axis: 1 - pos if step == OTHER else pos + step
            for axis, pos, step in zip(AXES, place, way)
        }

    def back(way):
        return tuple(step if step == OTHER else -step for step in way)

    def when_exists(way, act):
        there = exists(way)
        if there is None:
            act()
        else:
            pl.when(there)(act)

    ways = ways_of(sizes)
    messages = messages_of(sizes)
    z_steps = [way[2] for way in ways if way[0] == 0 and way[1] == 0 and way[2] != 0]

    xrx[...] = jnp.zeros_like(xrx)
    yrx[...] = jnp.zeros_like(yrx)
    xyrx[...] = jnp.zeros_like(xyrx)
    zrx[...] = jnp.zeros_like(zrx)

    barrier = pltpu.get_barrier_semaphore()
    for way in ways:
        def greet(way=way):
            pl.semaphore_signal(barrier, inc=1, device_id=device(way), device_id_type=MESH)

        when_exists(way, greet)

    def at_y(values, y):
        return values[:, y * cz : (y + 1) * cz]

    def over_y(make):
        return jnp.concatenate([make(y) for y in range(cy)], axis=1)

    for load in loads[:7]:
        load.wait()
    diagonal = iota((chans, chans), 0) == iota((chans, chans), 1)
    for source, target in ((bin_ref, bias_e), (bnode_ref, bias_n)):
        for layer in range(layers):
            row = source[layer : layer + 1, :]
            column = jnp.sum(jnp.where(diagonal, row, 0.0), axis=1, keepdims=True)
            target[layer] = jnp.broadcast_to(0.5 * column, (chans, cz))

    def halved(weights):
        return (0.5 * weights.astype(F32)).astype(BF16)

    fluid = mult_ref[1, 1:2, 1:2] > 0
    zeros = jnp.zeros((cy, cz), jnp.int32)
    for x in range(cx):
        count = mult_ref[x]
        ahead = (
            mult_ref[x + 1] if x < last else zeros,
            jnp.where(iota((cy, cz), 0) < cy - 1, pltpu.roll(count, cy - 1, 0), 0),
            jnp.where(iota((cy, cz), 1) < cz - 1, pltpu.roll(count, cz - 1, 1), 0),
        )
        for d in range(3):
            shared = jnp.minimum(count, ahead[d])
            weight = jnp.where(
                fluid & (shared > 0), 1.0 / jnp.maximum(shared, 1).astype(F32), 0.0
            )
            w_s[d, x] = over_y(lambda y: jnp.broadcast_to(weight[y : y + 1], (8, cz)))

    before_end = iota((chans, cz), 1) < cz - 1

    def keep_nodes(x, values):
        h_s[x] = values.astype(BF16)
        hz_s[x] = over_y(
            lambda y: jnp.where(before_end, pltpu.roll(at_y(values, y), cz - 1, 1), 0.0)
        ).astype(BF16)

    def channel_rows(index, values):
        stage_s[index] = values.astype(F32).reshape(rows, cz)
        return over_y(lambda y: stage_s[index, pl.ds(y, chans, stride=cy), :])

    loads[7].wait()
    for x in range(cx):
        keep_nodes(x, channel_rows(x, feat_ref[:, x]))
    loads[8].wait()
    for x in range(cx):
        for d in range(3):
            index = (1 + d) * cx + x
            e_s[d, x] = channel_rows(index, edge_ref[d, :, x]).astype(BF16)

    def next_nodes(x, d):
        if d == 2:
            return hz_s[x]
        if d == 1:
            return jnp.concatenate([h_s[x][:, cz:], jnp.zeros((chans, cz), BF16)], axis=1)
        return h_s[x + 1] if x < last else jnp.zeros((chans, cells), BF16)

    def edges(layer, slabs):
        weight_in, weight_out = halved(win_ref[layer]), wout_ref[layer]
        bias = jnp.concatenate([bias_e[layer]] * cy, axis=1)
        weighted = []
        for x, d in slabs:
            edge = e_s[d, x]
            stacked = jnp.concatenate([h_s[x], next_nodes(x, d), edge], axis=0)
            half = dot(weight_in, stacked) + bias
            message = dot(weight_out, silu_of_half(half).astype(BF16))
            e_s[d, x] = (edge.astype(F32) + message).astype(BF16)
            spread = message.reshape(chans // 8, 8, cells) * w_s[d, x][None]
            weighted.append(spread.reshape(chans, cells))
        return weighted

    def both_y(weighted):
        return weighted + jnp.concatenate(
            [jnp.zeros((chans, cz), F32), weighted[:, : cells - cz]], axis=1
        )

    def both_z(weighted):
        return weighted + over_y(lambda y: pltpu.roll(at_y(weighted, y), 1, 1))

    def put(slot, x, value, add):
        p_s[slot, x] = p_s[slot, x] + value if add else value

    def edge_lanes(side):
        return pl.ds(0 if side == 0 else cells - cz, cz)

    def transfer(message, slot, slow):
        way, tag = message
        dx, dy, dz = way
        index = messages.index(message)
        side = 0 if dy < 0 else 1
        face = 0 if dx < 0 else last
        if dz != 0:
            which = z_steps.index(dz)
            source = zsend.at[slot, which, SLOW if tag is None and face == slow else tag or FAST]
            target = zrx.at[slot, which, {-1: 0, 0: 1 + (tag or 0), 1: 3}[dx], dy + 1]
        elif dy == 0:
            source = p_s.at[slot, face]
            target = xrx.at[slot, 0 if dx < 0 else 1]
        elif dx == 0:
            slabs = pl.ds(last - slow, 1) if tag == FAST else pl.ds(0 if slow == 0 else 1, last)
            source = p_s.at[slot, slabs, :, edge_lanes(side)]
            target = yrx.at[slot, side, slabs]
        else:
            source = p_s.at[slot, face, :, edge_lanes(side)]
            target = xyrx.at[slot, (0 if dx < 0 else 2) + side]
        return pltpu.make_async_remote_copy(
            src_ref=source,
            dst_ref=target,
            send_sem=send_sem.at[slot, index],
            recv_sem=recv_sem.at[slot, index],
            device_id=device(way),
            device_id_type=MESH,
        )

    def start(message, slot, slow):
        when_exists(message[0], lambda: transfer(message, slot, slow).start())

    def arrive(message, slot, slow):
        when_exists(back(message[0]), lambda: transfer(message, slot, slow).wait_recv())

    def sent(message, slot, slow):
        when_exists(message[0], lambda: transfer(message, slot, slow).wait_send())

    lane = iota((128, cz), 1)
    odd_rows, even_rows = pl.ds(1, zrows, stride=2), pl.ds(0, zrows, stride=2)

    def z_faces(slot, xs, phase):
        faces = jnp.zeros((128, cz), F32)
        for x in xs:
            for part in range(halves):
                at = 2 * (x * halves + part)
                whole = p_s[slot, x]
                piece = jnp.concatenate(
                    [at_y(whole, part * per_half + y) for y in range(per_half)], axis=0
                )
                piece = pltpu.roll(piece, at + 1, 1)
                faces = jnp.where((lane == at) | (lane == at + 1), piece, faces)
        turn_s[2] = faces.T
        first, final = turn_s[2, odd_rows, :], turn_s[2, even_rows, :]
        for which, dz in enumerate(z_steps):
            if dz == OTHER:
                zsend[slot, which, phase] = jnp.where(place[2] == 0, final, first)
            else:
                zsend[slot, which, phase] = first if dz < 0 else final

    row_z, lane_z = iota((zrows, 128), 0), iota((zrows, 128), 1)

    def z_total(slot, which, face, phase):
        total = jnp.zeros((zrows, 128), F32)
        shift_x = last * halves
        for dy in STEPS:
            part = zrx[slot, which, 1 + phase, dy + 1]
            if face == 0:
                piece = zrx[slot, which, 3, dy + 1]
                piece = jnp.where(row_z < halves, pltpu.roll(piece, zrows - shift_x, 0), 0.0)
            else:
                piece = zrx[slot, which, 0, dy + 1]
                inside = (row_z >= shift_x) & (row_z < shift_x + halves)
                piece = jnp.where(inside, pltpu.roll(piece, shift_x, 0), 0.0)
            part = part + piece
            if dy > 0:
                part = pltpu.roll(pltpu.roll(part, chans % 128, 1), zrows - halves + 1, 0)
                part = jnp.where((row_z % halves == 0) & (lane_z < chans), part, 0.0)
            if dy < 0:
                part = pltpu.roll(pltpu.roll(part, 128 - chans, 1), halves - 1, 0)
                inside = (row_z % halves == halves - 1) & (lane_z >= 128 - chans)
                part = jnp.where(inside, part, 0.0)
            total = total + part
        return total

    def z_columns(slot, face, phase):
        for which, dz in enumerate(z_steps):
            total = z_total(slot, which, face, phase)
            if dz != 1:
                turn_s[phase, even_rows, :] = jnp.where(place[2] < sizes[2] - 1, total, 0.0)
            if dz != -1:
                turn_s[phase, odd_rows, :] = jnp.where(place[2] > 0, total, 0.0)
        return turn_s[phase].T

    def z_add(columns, x):
        out = []
        for part in range(halves):
            at = 2 * (x * halves + part)
            piece = pltpu.roll(columns, cz - at - 1, 1)
            out.append(jnp.where((lane == 0) | (lane == cz - 1), piece, 0.0))
        return over_y(
            lambda y: out[y // per_half][y % per_half * chans : (y % per_half + 1) * chans]
        )

    def node(layer, slot, x, columns):
        total = p_s[slot, x] + z_add(columns, x)
        if x == 0:
            total = total + xrx[slot, 1]
        if x == last:
            total = total + xrx[slot, 0]
        blocks = [at_y(total, y) for y in range(cy)]
        for side in range(2):
            extra = yrx[slot, 1 - side, x]
            if x == 0:
                extra = extra + xyrx[slot, 2 + (1 - side)]
            if x == last:
                extra = extra + xyrx[slot, 1 - side]
            blocks[-side] = blocks[-side] + extra
        incoming = jnp.concatenate(blocks, axis=1).astype(BF16)
        stacked = jnp.concatenate([h_s[x], incoming], axis=0)
        half = dot(halved(nin_ref[layer]), stacked)
        half = half + jnp.concatenate([bias_n[layer]] * cy, axis=1)
        step = dot(nout_ref[layer], silu_of_half(half).astype(BF16))
        return (h_s[x].astype(F32) + step).astype(BF16).astype(F32)

    turn_s[...] = jnp.zeros_like(turn_s)
    greetings = -1 + functools.reduce(
        lambda a, b: a * b,
        [
            1 + (pos > 0).astype(jnp.int32) + (pos < size - 1).astype(jnp.int32)
            for pos, size in zip(place, sizes)
        ],
    )
    middle = list(range(1, last))

    def run(slow):
        fast = last - slow

        def phase_of(message, sending):
            (dx, dy, dz), tag = message
            if dx != 0:
                face = 0 if (dx < 0) == sending else last
                return FAST if face == fast else SLOW
            return tag

        def order(message):
            (dx, dy, dz), tag = message
            return (dy != 0 or dz != 0, dz != 0)

        ordered = sorted(messages, key=order)

        def starts(slot, phase, first):
            for message in ordered:
                if phase_of(message, True) == phase and (order(message) == (False, False)) == first:
                    start(message, slot, slow)

        def arrivals(slot, phase, pick):
            for message in ordered:
                if phase_of(message, False) == phase and pick(message):
                    arrive(message, slot, slow)

        def shared_edge(face):
            return (0 if face == 0 else last - 1, 0)

        def own_edges(face):
            return ([(last, 0)] if face == last else []) + [(face, 2), (face, 1)]

        def inside(weighted):
            *absent, wz, wy = weighted
            return sum(absent, both_z(wz) + both_y(wy))

        def put_shared(slot, face, shared):
            put(slot, 1 if face == 0 else last - 1, shared, True)

        def fast_edges(layer):
            put(layer, fast, inside(edges(layer, own_edges(fast))), False)

        def middle_edges(layer):
            inner = [(x, 0) for x in middle[:-1]]
            for x in middle:
                put(layer, x, inside(edges(layer, [(x, 2), (x, 1)])), False)
            shared, *weighted = edges(layer, [shared_edge(fast)] + inner)
            for (x, d), value in zip(inner, weighted):
                put(layer, x, value, True)
                put(layer, x + 1, value, True)
            put(layer, fast, shared, True)
            put_shared(layer, fast, shared)

        def fast_sends(slot):
            starts(slot, FAST, True)
            z_faces(slot, [fast], FAST)
            starts(slot, FAST, False)

        fast_edges(0)
        middle_edges(0)
        pl.semaphore_wait(barrier, greetings)
        fast_sends(0)

        def layer_step(layer, carry):
            slot = layer
            shared, *weighted = edges(layer, [shared_edge(slow)] + own_edges(slow))
            put(slot, slow, shared + inside(weighted), False)
            starts(slot, SLOW, True)
            put_shared(slot, slow, shared)
            z_faces(slot, [slow] + middle, SLOW)
            starts(slot, SLOW, False)

            arrivals(slot, FAST, lambda message: True)
            columns = z_columns(slot, fast, FAST)
            keep_nodes(fast, node(layer, slot, fast, columns))

            @pl.when(layer + 1 < layers)
            def _():
                fast_edges(layer + 1)

            def late(message):
                (dx, dy, dz), tag = message
                return dz == 0 and dx != 0

            arrivals(slot, SLOW, lambda message: not late(message))
            columns = z_columns(slot, slow, SLOW)
            for x in middle:
                keep_nodes(x, node(layer, slot, x, columns))

            @pl.when(layer + 1 < layers)
            def _():
                middle_edges(layer + 1)
                fast_sends(layer + 1)

            for message in messages:
                sent(message, layer, slow)
            arrivals(slot, SLOW, late)
            keep_nodes(slow, node(layer, slot, slow, columns))
            return carry

        lax.fori_loop(0, layers, layer_step, 0)

    pl.when(lax.rem(place[0], 2) == 0)(lambda: run(0))
    pl.when(lax.rem(place[0], 2) == 1)(lambda: run(last))
    for x in range(cx):
        final = h_s[x].astype(F32)
        for y in range(cy):
            stage_s[x, pl.ds(y, chans, stride=cy), :] = at_y(final, y)
        out_ref[:, x] = stage_s[x].reshape(chans, cy, cz).astype(BF16)


def solution(mesh):
    sizes = tuple(mesh.shape[axis] for axis in AXES)

    def on_device(features, edge_state, multiplicity, *params):
        layers = params[0].shape[0]
        chans, cx, cy, cz = features.shape
        rows, cells = chans * cy, cy * cz
        assert cz == 128 and rows % 128 == 0 and cy % 8 == 0 and cx > 2
        assert chans % 16 == 0 and 128 % chans == 0 and cx * rows <= 64 * 128
        slots = layers
        ways = len(messages_of(sizes))
        zrows = -(-cx * (rows // 128) // 8) * 8
        vmem = pl.BlockSpec(memory_space=pltpu.VMEM)
        scratch = [pltpu.VMEM(a.shape, a.dtype) for a in (features, edge_state, multiplicity, *params)]
        scratch += [
            pltpu.VMEM((4 * cx, rows, cz), F32),
            pltpu.VMEM((cx, chans, cells), BF16),
            pltpu.VMEM((cx, chans, cells), BF16),
            pltpu.VMEM((3, cx, chans, cells), BF16),
            pltpu.VMEM((3, cx, 8, cells), F32),
            pltpu.VMEM((slots, cx, chans, cells), F32),
            pltpu.VMEM((layers, chans, cz), F32),
            pltpu.VMEM((layers, chans, cz), F32),
            pltpu.VMEM((slots, 2, 2, zrows, 128), F32),
            pltpu.VMEM((slots, 2, chans, cells), F32),
            pltpu.VMEM((slots, 2, cx, chans, cz), F32),
            pltpu.VMEM((slots, 4, chans, cz), F32),
            pltpu.VMEM((slots, 2, 4, 3, zrows, 128), F32),
            pltpu.VMEM((3, 128, 128), F32),
            pltpu.SemaphoreType.DMA((9,)),
            pltpu.SemaphoreType.DMA((slots, ways)),
            pltpu.SemaphoreType.DMA((slots, ways)),
        ]
        return pl.pallas_call(
            functools.partial(kernel, sizes, layers),
            out_shape=pltpu.VMEM(features.shape, features.dtype),
            in_specs=[pl.BlockSpec(memory_space=pltpu.HBM)] * 9,
            out_specs=vmem,
            scratch_shapes=scratch,
            compiler_params=pltpu.CompilerParams(
                collective_id=0, has_side_effects=True, vmem_limit_bytes=60 * 1024 * 1024
            ),
        )(features, edge_state, multiplicity, *params)

    placed = (P(None, *AXES), P(None, None, *AXES), P(*AXES)) + (P(),) * 6
    return jax.shard_map(
        on_device, mesh=mesh, in_specs=placed, out_specs=P(None, *AXES), check_vma=False
    )
```

```python
import functools
import itertools

import jax
import jax.numpy as jnp
from jax import lax
from jax.experimental import pallas as pl
from jax.experimental.pallas import tpu as pltpu
from jax.sharding import PartitionSpec as P

MESH = pl.DeviceIdType.MESH
AXES = ("gx", "gy", "gz")
F32, BF16 = jnp.float32, jnp.bfloat16
STEPS = (-1, 0, 1)
FAST, SLOW, MID = 0, 1, 2
OTHER = 2


def iota(shape, dim):
    return lax.broadcasted_iota(jnp.int32, shape, dim)


def dot(a, b):
    return jnp.dot(a, b, preferred_element_type=F32)


def silu_of_half(half):
    return half + half * jnp.tanh(half)


def ways_of(sizes):
    z_steps = {1: (0,), 2: (0, OTHER)}.get(sizes[2], STEPS)
    ways = itertools.product(STEPS, STEPS, z_steps)
    return [
        way for way in ways if any(way) and all(s == 0 or n > 1 for s, n in zip(way, sizes))
    ]


def messages_of(sizes):
    out = []
    for way in ways_of(sizes):
        dx, dy, dz = way
        out += [(way, tag) for tag in ((FAST, SLOW, MID) if dx == 0 else (None,))]
    return out


def kernel(
    sizes,
    layers,
    feat_hbm, edge_hbm, mult_hbm, win_hbm, wout_hbm, bin_hbm, nin_hbm, nout_hbm, bnode_hbm,
    out_ref,
    feat_ref, edge_ref, mult_ref, win_ref, wout_ref, bin_ref, nin_ref, nout_ref, bnode_ref,
    stage_s, h_s, hz_s, e_s, w_s, p_s, bias_e, bias_n,
    zsend, xrx, yrx, xyrx, zrx, turn_s, in_sem, send_sem, recv_sem,
):
    loads = [
        pltpu.make_async_copy(source, target, in_sem.at[index])
        for index, (source, target) in enumerate([
            (win_hbm, win_ref), (wout_hbm, wout_ref), (bin_hbm, bin_ref), (nin_hbm, nin_ref),
            (nout_hbm, nout_ref), (bnode_hbm, bnode_ref), (mult_hbm, mult_ref),
            (feat_hbm, feat_ref), (edge_hbm, edge_ref),
        ])
    ]
    for load in loads:
        load.start()

    chans, cx, cy, cz = feat_ref.shape
    rows, cells = chans * cy, cy * cz
    halves = rows // 128
    per_half = cy // halves
    last = cx - 1
    zrows = zsend.shape[3]
    place = [lax.axis_index(axis) for axis in AXES]

    def exists(way):
        there = None
        for pos, step, size in zip(place, way, sizes):
            if step == 0 or step == OTHER:
                continue
            here = pos > 0 if step < 0 else pos < size - 1
            there = here if there is None else there & here
        return there

    def device(way):
        return {
            axis: 1 - pos if step == OTHER else pos + step
            for axis, pos, step in zip(AXES, place, way)
        }

    def back(way):
        return tuple(step if step == OTHER else -step for step in way)

    def when_exists(way, act):
        there = exists(way)
        if there is None:
            act()
        else:
            pl.when(there)(act)

    ways = ways_of(sizes)
    messages = messages_of(sizes)
    z_steps = [way[2] for way in ways if way[0] == 0 and way[1] == 0 and way[2] != 0]

    xrx[...] = jnp.zeros_like(xrx)
    yrx[...] = jnp.zeros_like(yrx)
    xyrx[...] = jnp.zeros_like(xyrx)
    zrx[...] = jnp.zeros_like(zrx)

    barrier = pltpu.get_barrier_semaphore()
    for way in ways:
        def greet(way=way):
            pl.semaphore_signal(barrier, inc=1, device_id=device(way), device_id_type=MESH)

        when_exists(way, greet)

    def at_y(values, y):
        return values[:, y * cz : (y + 1) * cz]

    def over_y(make):
        return jnp.concatenate([make(y) for y in range(cy)], axis=1)

    for load in loads[:7]:
        load.wait()
    diagonal = iota((chans, chans), 0) == iota((chans, chans), 1)
    for source, target in ((bin_ref, bias_e), (bnode_ref, bias_n)):
        for layer in range(layers):
            row = source[layer : layer + 1, :]
            column = jnp.sum(jnp.where(diagonal, row, 0.0), axis=1, keepdims=True)
            target[layer] = jnp.broadcast_to(0.5 * column, (chans, cz))

    def halved(weights):
        return (0.5 * weights.astype(F32)).astype(BF16)

    fluid = mult_ref[1, 1:2, 1:2] > 0
    zeros = jnp.zeros((cy, cz), jnp.int32)
    for x in range(cx):
        count = mult_ref[x]
        ahead = (
            mult_ref[x + 1] if x < last else zeros,
            jnp.where(iota((cy, cz), 0) < cy - 1, pltpu.roll(count, cy - 1, 0), 0),
            jnp.where(iota((cy, cz), 1) < cz - 1, pltpu.roll(count, cz - 1, 1), 0),
        )
        for d in range(3):
            shared = jnp.minimum(count, ahead[d])
            weight = jnp.where(
                fluid & (shared > 0), 1.0 / jnp.maximum(shared, 1).astype(F32), 0.0
            )
            w_s[d, x] = over_y(lambda y: jnp.broadcast_to(weight[y : y + 1], (8, cz)))

    before_end = iota((chans, cz), 1) < cz - 1

    def keep_nodes(x, values):
        h_s[x] = values.astype(BF16)
        hz_s[x] = over_y(
            lambda y: jnp.where(before_end, pltpu.roll(at_y(values, y), cz - 1, 1), 0.0)
        ).astype(BF16)

    def channel_rows(index, values):
        stage_s[index] = values.astype(F32).reshape(rows, cz)
        return over_y(lambda y: stage_s[index, pl.ds(y, chans, stride=cy), :])

    loads[7].wait()
    for x in range(cx):
        keep_nodes(x, channel_rows(x, feat_ref[:, x]))
    loads[8].wait()
    for x in range(cx):
        for d in range(3):
            index = (1 + d) * cx + x
            e_s[d, x] = channel_rows(index, edge_ref[d, :, x]).astype(BF16)

    def next_nodes(x, d):
        if d == 2:
            return hz_s[x]
        if d == 1:
            return jnp.concatenate([h_s[x][:, cz:], jnp.zeros((chans, cz), BF16)], axis=1)
        return h_s[x + 1] if x < last else jnp.zeros((chans, cells), BF16)

    def edges(layer, slabs):
        weight_in, weight_out = halved(win_ref[layer]), wout_ref[layer]
        bias = jnp.concatenate([bias_e[layer]] * cy, axis=1)
        weighted = []
        for x, d in slabs:
            edge = e_s[d, x]
            stacked = jnp.concatenate([h_s[x], next_nodes(x, d), edge], axis=0)
            half = dot(weight_in, stacked) + bias
            message = dot(weight_out, silu_of_half(half).astype(BF16))
            e_s[d, x] = (edge.astype(F32) + message).astype(BF16)
            spread = message.reshape(chans // 8, 8, cells) * w_s[d, x][None]
            weighted.append(spread.reshape(chans, cells))
        return weighted

    def both_y(weighted):
        return weighted + jnp.concatenate(
            [jnp.zeros((chans, cz), F32), weighted[:, : cells - cz]], axis=1
        )

    def both_z(weighted):
        return weighted + over_y(lambda y: pltpu.roll(at_y(weighted, y), 1, 1))

    def put(slot, x, value, add):
        p_s[slot, x] = p_s[slot, x] + value if add else value

    def edge_lanes(side):
        return pl.ds(0 if side == 0 else cells - cz, cz)

    def transfer(message, slot, slow):
        way, tag = message
        dx, dy, dz = way
        index = messages.index(message)
        side = 0 if dy < 0 else 1
        face = 0 if dx < 0 else last
        if dz != 0:
            which = z_steps.index(dz)
            source = zsend.at[slot, which, SLOW if tag is None and face == slow else tag or FAST]
            target = zrx.at[slot, which, {-1: 0, 0: 1 + (tag or 0), 1: 4}[dx], dy + 1]
        elif dy == 0:
            source = p_s.at[slot, face]
            target = xrx.at[slot, 0 if dx < 0 else 1]
        elif dx == 0:
            slabs = {FAST: (last - slow, 1), SLOW: (slow, 1), MID: (1, last - 1)}[tag]
            slabs = pl.ds(*slabs)
            source = p_s.at[slot, slabs, :, edge_lanes(side)]
            target = yrx.at[slot, side, slabs]
        else:
            source = p_s.at[slot, face, :, edge_lanes(side)]
            target = xyrx.at[slot, (0 if dx < 0 else 2) + side]
        return pltpu.make_async_remote_copy(
            src_ref=source,
            dst_ref=target,
            send_sem=send_sem.at[slot, index],
            recv_sem=recv_sem.at[slot, index],
            device_id=device(way),
            device_id_type=MESH,
        )

    def start(message, slot, slow):
        when_exists(message[0], lambda: transfer(message, slot, slow).start())

    def arrive(message, slot, slow):
        when_exists(back(message[0]), lambda: transfer(message, slot, slow).wait_recv())

    def sent(message, slot, slow):
        when_exists(message[0], lambda: transfer(message, slot, slow).wait_send())

    lane = iota((128, cz), 1)
    odd_rows, even_rows = pl.ds(1, zrows, stride=2), pl.ds(0, zrows, stride=2)

    def z_faces(slot, xs, phase):
        faces = jnp.zeros((128, cz), F32)
        for x in xs:
            for part in range(halves):
                at = 2 * (x * halves + part)
                whole = p_s[slot, x]
                piece = jnp.concatenate(
                    [at_y(whole, part * per_half + y) for y in range(per_half)], axis=0
                )
                piece = pltpu.roll(piece, at + 1, 1)
                faces = jnp.where((lane == at) | (lane == at + 1), piece, faces)
        turn_s[3] = faces.T
        first, final = turn_s[3, odd_rows, :], turn_s[3, even_rows, :]
        for which, dz in enumerate(z_steps):
            if dz == OTHER:
                zsend[slot, which, phase] = jnp.where(place[2] == 0, final, first)
            else:
                zsend[slot, which, phase] = first if dz < 0 else final

    row_z, lane_z = iota((zrows, 128), 0), iota((zrows, 128), 1)

    def z_total(slot, which, face, phase):
        total = jnp.zeros((zrows, 128), F32)
        shift_x = last * halves
        for dy in STEPS:
            part = zrx[slot, which, 1 + phase, dy + 1]
            piece = 0.0
            if face == 0:
                piece = zrx[slot, which, 4, dy + 1]
                piece = jnp.where(row_z < halves, pltpu.roll(piece, zrows - shift_x, 0), 0.0)
            elif face == last:
                piece = zrx[slot, which, 0, dy + 1]
                inside = (row_z >= shift_x) & (row_z < shift_x + halves)
                piece = jnp.where(inside, pltpu.roll(piece, shift_x, 0), 0.0)
            part = part + piece
            if dy > 0:
                part = pltpu.roll(pltpu.roll(part, chans % 128, 1), zrows - halves + 1, 0)
                part = jnp.where((row_z % halves == 0) & (lane_z < chans), part, 0.0)
            if dy < 0:
                part = pltpu.roll(pltpu.roll(part, 128 - chans, 1), halves - 1, 0)
                inside = (row_z % halves == halves - 1) & (lane_z >= 128 - chans)
                part = jnp.where(inside, part, 0.0)
            total = total + part
        return total

    def z_columns(slot, face, phase):
        for which, dz in enumerate(z_steps):
            total = z_total(slot, which, face, phase)
            if dz != 1:
                turn_s[phase, even_rows, :] = jnp.where(place[2] < sizes[2] - 1, total, 0.0)
            if dz != -1:
                turn_s[phase, odd_rows, :] = jnp.where(place[2] > 0, total, 0.0)
        return turn_s[phase].T

    def z_add(columns, x):
        out = []
        for part in range(halves):
            at = 2 * (x * halves + part)
            piece = pltpu.roll(columns, cz - at - 1, 1)
            out.append(jnp.where((lane == 0) | (lane == cz - 1), piece, 0.0))
        return over_y(
            lambda y: out[y // per_half][y % per_half * chans : (y % per_half + 1) * chans]
        )

    def node(layer, slot, x, columns):
        total = p_s[slot, x] + z_add(columns, x)
        if x == 0:
            total = total + xrx[slot, 1]
        if x == last:
            total = total + xrx[slot, 0]
        blocks = [at_y(total, y) for y in range(cy)]
        for side in range(2):
            extra = yrx[slot, 1 - side, x]
            if x == 0:
                extra = extra + xyrx[slot, 2 + (1 - side)]
            if x == last:
                extra = extra + xyrx[slot, 1 - side]
            blocks[-side] = blocks[-side] + extra
        incoming = jnp.concatenate(blocks, axis=1).astype(BF16)
        stacked = jnp.concatenate([h_s[x], incoming], axis=0)
        half = dot(halved(nin_ref[layer]), stacked)
        half = half + jnp.concatenate([bias_n[layer]] * cy, axis=1)
        step = dot(nout_ref[layer], silu_of_half(half).astype(BF16))
        return (h_s[x].astype(F32) + step).astype(BF16).astype(F32)

    turn_s[...] = jnp.zeros_like(turn_s)
    greetings = -1 + functools.reduce(
        lambda a, b: a * b,
        [
            1 + (pos > 0).astype(jnp.int32) + (pos < size - 1).astype(jnp.int32)
            for pos, size in zip(place, sizes)
        ],
    )
    middle = list(range(1, last))

    def run(slow):
        fast = last - slow

        def phase_of(message, sending):
            (dx, dy, dz), tag = message
            if dx != 0:
                face = 0 if (dx < 0) == sending else last
                return FAST if face == fast else SLOW
            return tag

        def order(message):
            (dx, dy, dz), tag = message
            return (dy != 0 or dz != 0, dz != 0)

        ordered = sorted(messages, key=order)

        def starts(slot, phase, first):
            for message in ordered:
                if phase_of(message, True) == phase and (order(message) == (False, False)) == first:
                    start(message, slot, slow)

        def arrivals(slot, phase):
            for message in ordered:
                if phase_of(message, False) == phase:
                    arrive(message, slot, slow)

        def shared_edge(face):
            return (0 if face == 0 else last - 1, 0)

        def own_edges(face):
            return ([(last, 0)] if face == last else []) + [(face, 2), (face, 1)]

        def inside(weighted):
            *absent, wz, wy = weighted
            return sum(absent, both_z(wz) + both_y(wy))

        def put_shared(slot, face, shared):
            put(slot, 1 if face == 0 else last - 1, shared, True)

        def fast_edges(layer):
            put(layer, fast, inside(edges(layer, own_edges(fast))), False)

        def middle_edges(layer):
            inner = [(x, 0) for x in middle[:-1]]
            for x in middle:
                put(layer, x, inside(edges(layer, [(x, 2), (x, 1)])), False)
            shared, *weighted = edges(layer, [shared_edge(fast)] + inner)
            for (x, d), value in zip(inner, weighted):
                put(layer, x, value, True)
                put(layer, x + 1, value, True)
            put(layer, fast, shared, True)
            put_shared(layer, fast, shared)

        def fast_sends(slot):
            starts(slot, FAST, True)
            z_faces(slot, [fast], FAST)
            starts(slot, FAST, False)

        fast_edges(0)
        middle_edges(0)
        pl.semaphore_wait(barrier, greetings)
        fast_sends(0)

        def layer_step(layer, carry):
            slot = layer
            (shared,) = edges(layer, [shared_edge(slow)])
            put_shared(slot, slow, shared)
            z_faces(slot, middle, MID)
            starts(slot, MID, False)
            put(slot, slow, shared + inside(edges(layer, own_edges(slow))), False)
            starts(slot, SLOW, True)
            z_faces(slot, [slow], SLOW)
            starts(slot, SLOW, False)

            arrivals(slot, FAST)
            columns = z_columns(slot, fast, FAST)
            keep_nodes(fast, node(layer, slot, fast, columns))

            @pl.when(layer + 1 < layers)
            def _():
                fast_edges(layer + 1)

            arrivals(slot, MID)
            columns = z_columns(slot, None, MID)
            for x in middle:
                keep_nodes(x, node(layer, slot, x, columns))

            @pl.when(layer + 1 < layers)
            def _():
                middle_edges(layer + 1)
                fast_sends(layer + 1)

            for message in messages:
                sent(message, layer, slow)
            arrivals(slot, SLOW)
            columns = z_columns(slot, slow, SLOW)
            keep_nodes(slow, node(layer, slot, slow, columns))
            return carry

        lax.fori_loop(0, layers, layer_step, 0)

    pl.when(lax.rem(place[0], 2) == 0)(lambda: run(0))
    pl.when(lax.rem(place[0], 2) == 1)(lambda: run(last))
    for x in range(cx):
        final = h_s[x].astype(F32)
        for y in range(cy):
            stage_s[x, pl.ds(y, chans, stride=cy), :] = at_y(final, y)
        out_ref[:, x] = stage_s[x].reshape(chans, cy, cz).astype(BF16)


def solution(mesh):
    sizes = tuple(mesh.shape[axis] for axis in AXES)

    def on_device(features, edge_state, multiplicity, *params):
        layers = params[0].shape[0]
        chans, cx, cy, cz = features.shape
        rows, cells = chans * cy, cy * cz
        assert cz == 128 and rows % 128 == 0 and cy % 8 == 0 and cx > 2
        assert chans % 16 == 0 and 128 % chans == 0 and cx * rows <= 64 * 128
        slots = layers
        ways = len(messages_of(sizes))
        zrows = -(-cx * (rows // 128) // 8) * 8
        vmem = pl.BlockSpec(memory_space=pltpu.VMEM)
        scratch = [pltpu.VMEM(a.shape, a.dtype) for a in (features, edge_state, multiplicity, *params)]
        scratch += [
            pltpu.VMEM((4 * cx, rows, cz), F32),
            pltpu.VMEM((cx, chans, cells), BF16),
            pltpu.VMEM((cx, chans, cells), BF16),
            pltpu.VMEM((3, cx, chans, cells), BF16),
            pltpu.VMEM((3, cx, 8, cells), F32),
            pltpu.VMEM((slots, cx, chans, cells), F32),
            pltpu.VMEM((layers, chans, cz), F32),
            pltpu.VMEM((layers, chans, cz), F32),
            pltpu.VMEM((slots, 2, 3, zrows, 128), F32),
            pltpu.VMEM((slots, 2, chans, cells), F32),
            pltpu.VMEM((slots, 2, cx, chans, cz), F32),
            pltpu.VMEM((slots, 4, chans, cz), F32),
            pltpu.VMEM((slots, 2, 5, 3, zrows, 128), F32),
            pltpu.VMEM((4, 128, 128), F32),
            pltpu.SemaphoreType.DMA((9,)),
            pltpu.SemaphoreType.DMA((slots, ways)),
            pltpu.SemaphoreType.DMA((slots, ways)),
        ]
        return pl.pallas_call(
            functools.partial(kernel, sizes, layers),
            out_shape=pltpu.VMEM(features.shape, features.dtype),
            in_specs=[pl.BlockSpec(memory_space=pltpu.HBM)] * 9,
            out_specs=vmem,
            scratch_shapes=scratch,
            compiler_params=pltpu.CompilerParams(
                collective_id=0, has_side_effects=True, vmem_limit_bytes=60 * 1024 * 1024
            ),
        )(features, edge_state, multiplicity, *params)

    placed = (P(None, *AXES), P(None, None, *AXES), P(*AXES)) + (P(),) * 6
    return jax.shard_map(
        on_device, mesh=mesh, in_specs=placed, out_specs=P(None, *AXES), check_vma=False
    )
```

```python
import functools
import itertools

import jax
import jax.numpy as jnp
from jax import lax
from jax.experimental import pallas as pl
from jax.experimental.pallas import tpu as pltpu
from jax.sharding import PartitionSpec as P

MESH = pl.DeviceIdType.MESH
AXES = ("gx", "gy", "gz")
F32, BF16 = jnp.float32, jnp.bfloat16
STEPS = (-1, 0, 1)
FAST, SLOW, MID = 0, 1, 2
OTHER = 2


def iota(shape, dim):
    return lax.broadcasted_iota(jnp.int32, shape, dim)


def dot(a, b):
    return jnp.dot(a, b, preferred_element_type=F32)


def silu_of_half(half):
    return half + half * jnp.tanh(half)


def ways_of(sizes):
    z_steps = {1: (0,), 2: (0, OTHER)}.get(sizes[2], STEPS)
    ways = itertools.product(STEPS, STEPS, z_steps)
    return [
        way for way in ways if any(way) and all(s == 0 or n > 1 for s, n in zip(way, sizes))
    ]


def messages_of(sizes):
    out = []
    for way in ways_of(sizes):
        dx, dy, dz = way
        out += [(way, tag) for tag in ((FAST, SLOW, MID) if dx == 0 else (None,))]
    return out


def kernel(
    sizes,
    layers,
    feat_hbm, edge_hbm, mult_hbm, win_hbm, wout_hbm, bin_hbm, nin_hbm, nout_hbm, bnode_hbm,
    out_ref,
    feat_ref, edge_ref, mult_ref, win_ref, wout_ref, bin_ref, nin_ref, nout_ref, bnode_ref,
    stage_s, h_s, hz_s, e_s, w_s, p_s, bias_e, bias_n,
    zsend, xrx, yrx, xyrx, zrx, turn_s, in_sem, send_sem, recv_sem,
):
    loads = [
        pltpu.make_async_copy(source, target, in_sem.at[index])
        for index, (source, target) in enumerate([
            (win_hbm, win_ref), (wout_hbm, wout_ref), (bin_hbm, bin_ref), (nin_hbm, nin_ref),
            (nout_hbm, nout_ref), (bnode_hbm, bnode_ref), (mult_hbm, mult_ref),
            (feat_hbm, feat_ref), (edge_hbm, edge_ref),
        ])
    ]
    for load in loads:
        load.start()

    chans, cx, cy, cz = feat_ref.shape
    rows, cells = chans * cy, cy * cz
    halves = rows // 128
    per_half = cy // halves
    last = cx - 1
    zrows = zsend.shape[3]
    place = [lax.axis_index(axis) for axis in AXES]

    def exists(way):
        there = None
        for pos, step, size in zip(place, way, sizes):
            if step == 0 or step == OTHER:
                continue
            here = pos > 0 if step < 0 else pos < size - 1
            there = here if there is None else there & here
        return there

    def device(way):
        return {
            axis: 1 - pos if step == OTHER else pos + step
            for axis, pos, step in zip(AXES, place, way)
        }

    def back(way):
        return tuple(step if step == OTHER else -step for step in way)

    def when_exists(way, act):
        there = exists(way)
        if there is None:
            act()
        else:
            pl.when(there)(act)

    ways = ways_of(sizes)
    messages = messages_of(sizes)
    z_steps = [way[2] for way in ways if way[0] == 0 and way[1] == 0 and way[2] != 0]

    xrx[...] = jnp.zeros_like(xrx)
    yrx[...] = jnp.zeros_like(yrx)
    xyrx[...] = jnp.zeros_like(xyrx)
    zrx[...] = jnp.zeros_like(zrx)

    barrier = pltpu.get_barrier_semaphore()
    for way in ways:
        def greet(way=way):
            pl.semaphore_signal(barrier, inc=1, device_id=device(way), device_id_type=MESH)

        when_exists(way, greet)

    def at_y(values, y):
        return values[:, y * cz : (y + 1) * cz]

    def over_y(make):
        return jnp.concatenate([make(y) for y in range(cy)], axis=1)

    for load in loads[:7]:
        load.wait()
    diagonal = iota((chans, chans), 0) == iota((chans, chans), 1)
    for source, target in ((bin_ref, bias_e), (bnode_ref, bias_n)):
        for layer in range(layers):
            row = source[layer : layer + 1, :]
            column = jnp.sum(jnp.where(diagonal, row, 0.0), axis=1, keepdims=True)
            target[layer] = jnp.broadcast_to(0.5 * column, (chans, cz))

    def halved(weights):
        return (0.5 * weights.astype(F32)).astype(BF16)

    fluid = mult_ref[1, 1:2, 1:2] > 0
    zeros = jnp.zeros((cy, cz), jnp.int32)
    for x in range(cx):
        count = mult_ref[x]
        ahead = (
            mult_ref[x + 1] if x < last else zeros,
            jnp.where(iota((cy, cz), 0) < cy - 1, pltpu.roll(count, cy - 1, 0), 0),
            jnp.where(iota((cy, cz), 1) < cz - 1, pltpu.roll(count, cz - 1, 1), 0),
        )
        for d in range(3):
            shared = jnp.minimum(count, ahead[d])
            weight = jnp.where(
                fluid & (shared > 0), 1.0 / jnp.maximum(shared, 1).astype(F32), 0.0
            )
            w_s[d, x] = over_y(lambda y: jnp.broadcast_to(weight[y : y + 1], (8, cz)))

    before_end = iota((chans, cz), 1) < cz - 1

    def keep_nodes(x, values):
        h_s[x] = values.astype(BF16)
        hz_s[x] = over_y(
            lambda y: jnp.where(before_end, pltpu.roll(at_y(values, y), cz - 1, 1), 0.0)
        ).astype(BF16)

    def channel_rows(index, values):
        stage_s[index] = values.astype(F32).reshape(rows, cz)
        return over_y(lambda y: stage_s[index, pl.ds(y, chans, stride=cy), :])

    loads[7].wait()
    for x in range(cx):
        keep_nodes(x, channel_rows(x, feat_ref[:, x]))
    loads[8].wait()
    for x in range(cx):
        for d in range(3):
            index = (1 + d) * cx + x
            e_s[d, x] = channel_rows(index, edge_ref[d, :, x]).astype(BF16)

    def next_nodes(x, d):
        if d == 2:
            return hz_s[x]
        if d == 1:
            return jnp.concatenate([h_s[x][:, cz:], jnp.zeros((chans, cz), BF16)], axis=1)
        return h_s[x + 1] if x < last else jnp.zeros((chans, cells), BF16)

    def edges(layer, slabs):
        weight_in, weight_out = halved(win_ref[layer]), wout_ref[layer]
        bias = jnp.concatenate([bias_e[layer]] * cy, axis=1)
        weighted = []
        for x, d in slabs:
            edge = e_s[d, x]
            stacked = jnp.concatenate([h_s[x], next_nodes(x, d), edge], axis=0)
            half = dot(weight_in, stacked) + bias
            message = dot(weight_out, silu_of_half(half).astype(BF16))
            e_s[d, x] = (edge.astype(F32) + message).astype(BF16)
            spread = message.reshape(chans // 8, 8, cells) * w_s[d, x][None]
            weighted.append(spread.reshape(chans, cells))
        return weighted

    def both_y(weighted):
        return weighted + jnp.concatenate(
            [jnp.zeros((chans, cz), F32), weighted[:, : cells - cz]], axis=1
        )

    def both_z(weighted):
        return weighted + over_y(lambda y: pltpu.roll(at_y(weighted, y), 1, 1))

    def put(slot, x, value, add):
        p_s[slot, x] = p_s[slot, x] + value if add else value

    def edge_lanes(side):
        return pl.ds(0 if side == 0 else cells - cz, cz)

    def transfer(message, slot, slow):
        way, tag = message
        dx, dy, dz = way
        index = messages.index(message)
        side = 0 if dy < 0 else 1
        face = 0 if dx < 0 else last
        if dz != 0:
            which = z_steps.index(dz)
            source = zsend.at[slot, which, SLOW if tag is None and face == slow else tag or FAST]
            target = zrx.at[slot, which, {-1: 0, 0: 1 + (tag or 0), 1: 4}[dx], dy + 1]
        elif dy == 0:
            source = p_s.at[slot, face]
            target = xrx.at[slot, 0 if dx < 0 else 1]
        elif dx == 0:
            slabs = {FAST: (last - slow, 1), SLOW: (slow, 1), MID: (1, last - 1)}[tag]
            slabs = pl.ds(*slabs)
            source = p_s.at[slot, slabs, :, edge_lanes(side)]
            target = yrx.at[slot, side, slabs]
        else:
            source = p_s.at[slot, face, :, edge_lanes(side)]
            target = xyrx.at[slot, (0 if dx < 0 else 2) + side]
        return pltpu.make_async_remote_copy(
            src_ref=source,
            dst_ref=target,
            send_sem=send_sem.at[slot, index],
            recv_sem=recv_sem.at[slot, index],
            device_id=device(way),
            device_id_type=MESH,
        )

    def start(message, slot, slow):
        when_exists(message[0], lambda: transfer(message, slot, slow).start())

    def arrive(message, slot, slow):
        when_exists(back(message[0]), lambda: transfer(message, slot, slow).wait_recv())

    def sent(message, slot, slow):
        when_exists(message[0], lambda: transfer(message, slot, slow).wait_send())

    lane = iota((128, cz), 1)
    odd_rows, even_rows = pl.ds(1, zrows, stride=2), pl.ds(0, zrows, stride=2)

    def z_faces(slot, xs, phase):
        faces = jnp.zeros((128, cz), F32)
        for x in xs:
            for part in range(halves):
                at = 2 * (x * halves + part)
                whole = p_s[slot, x]
                piece = jnp.concatenate(
                    [at_y(whole, part * per_half + y) for y in range(per_half)], axis=0
                )
                piece = pltpu.roll(piece, at + 1, 1)
                faces = jnp.where((lane == at) | (lane == at + 1), piece, faces)
        turn_s[3] = faces.T
        first, final = turn_s[3, odd_rows, :], turn_s[3, even_rows, :]
        for which, dz in enumerate(z_steps):
            if dz == OTHER:
                zsend[slot, which, phase] = jnp.where(place[2] == 0, final, first)
            else:
                zsend[slot, which, phase] = first if dz < 0 else final

    row_z, lane_z = iota((zrows, 128), 0), iota((zrows, 128), 1)

    def z_total(slot, which, face, phase):
        total = jnp.zeros((zrows, 128), F32)
        shift_x = last * halves
        for dy in STEPS:
            part = zrx[slot, which, 1 + phase, dy + 1]
            piece = 0.0
            if face == 0:
                piece = zrx[slot, which, 4, dy + 1]
                piece = jnp.where(row_z < halves, pltpu.roll(piece, zrows - shift_x, 0), 0.0)
            elif face == last:
                piece = zrx[slot, which, 0, dy + 1]
                inside = (row_z >= shift_x) & (row_z < shift_x + halves)
                piece = jnp.where(inside, pltpu.roll(piece, shift_x, 0), 0.0)
            part = part + piece
            if dy > 0:
                part = pltpu.roll(pltpu.roll(part, chans % 128, 1), zrows - halves + 1, 0)
                part = jnp.where((row_z % halves == 0) & (lane_z < chans), part, 0.0)
            if dy < 0:
                part = pltpu.roll(pltpu.roll(part, 128 - chans, 1), halves - 1, 0)
                inside = (row_z % halves == halves - 1) & (lane_z >= 128 - chans)
                part = jnp.where(inside, part, 0.0)
            total = total + part
        return total

    def z_columns(slot, face, phase):
        for which, dz in enumerate(z_steps):
            total = z_total(slot, which, face, phase)
            if dz != 1:
                turn_s[phase, even_rows, :] = jnp.where(place[2] < sizes[2] - 1, total, 0.0)
            if dz != -1:
                turn_s[phase, odd_rows, :] = jnp.where(place[2] > 0, total, 0.0)
        return turn_s[phase].T

    def z_add(columns, x):
        out = []
        for part in range(halves):
            at = 2 * (x * halves + part)
            piece = pltpu.roll(columns, cz - at - 1, 1)
            out.append(jnp.where((lane == 0) | (lane == cz - 1), piece, 0.0))
        return over_y(
            lambda y: out[y // per_half][y % per_half * chans : (y % per_half + 1) * chans]
        )

    def node(layer, slot, x, columns):
        total = p_s[slot, x] + z_add(columns, x)
        if x == 0:
            total = total + xrx[slot, 1]
        if x == last:
            total = total + xrx[slot, 0]
        blocks = [at_y(total, y) for y in range(cy)]
        for side in range(2):
            extra = yrx[slot, 1 - side, x]
            if x == 0:
                extra = extra + xyrx[slot, 2 + (1 - side)]
            if x == last:
                extra = extra + xyrx[slot, 1 - side]
            blocks[-side] = blocks[-side] + extra
        incoming = jnp.concatenate(blocks, axis=1).astype(BF16)
        stacked = jnp.concatenate([h_s[x], incoming], axis=0)
        half = dot(halved(nin_ref[layer]), stacked)
        half = half + jnp.concatenate([bias_n[layer]] * cy, axis=1)
        step = dot(nout_ref[layer], silu_of_half(half).astype(BF16))
        return (h_s[x].astype(F32) + step).astype(BF16).astype(F32)

    turn_s[...] = jnp.zeros_like(turn_s)
    greetings = -1 + functools.reduce(
        lambda a, b: a * b,
        [
            1 + (pos > 0).astype(jnp.int32) + (pos < size - 1).astype(jnp.int32)
            for pos, size in zip(place, sizes)
        ],
    )
    middle = list(range(1, last))

    def run(slow):
        fast = last - slow

        def phase_of(message, sending):
            (dx, dy, dz), tag = message
            if dx != 0:
                face = 0 if (dx < 0) == sending else last
                return FAST if face == fast else SLOW
            return tag

        def order(message):
            (dx, dy, dz), tag = message
            hops = sum(step != 0 for step in (dx, dy, dz))
            return (dz == 0, dz == 0 and dy != 0, -hops)

        ordered = sorted(messages, key=order)

        def starts(slot, phase):
            for message in ordered:
                if phase_of(message, True) == phase:
                    start(message, slot, slow)

        def arrivals(slot, phase):
            for message in ordered:
                if phase_of(message, False) == phase:
                    arrive(message, slot, slow)

        def shared_edge(face):
            return (0 if face == 0 else last - 1, 0)

        def own_edges(face):
            return ([(last, 0)] if face == last else []) + [(face, 2), (face, 1)]

        def inside(weighted):
            *absent, wz, wy = weighted
            return sum(absent, both_z(wz) + both_y(wy))

        def put_shared(slot, face, shared):
            put(slot, 1 if face == 0 else last - 1, shared, True)

        def fast_edges(layer):
            put(layer, fast, inside(edges(layer, own_edges(fast))), False)

        def middle_edges(layer):
            inner = [(x, 0) for x in middle[:-1]]
            for x in middle:
                put(layer, x, inside(edges(layer, [(x, 2), (x, 1)])), False)
            shared, *weighted = edges(layer, [shared_edge(fast)] + inner)
            for (x, d), value in zip(inner, weighted):
                put(layer, x, value, True)
                put(layer, x + 1, value, True)
            put(layer, fast, shared, True)
            put_shared(layer, fast, shared)

        def fast_sends(slot):
            z_faces(slot, [fast], FAST)
            starts(slot, FAST)

        fast_edges(0)
        middle_edges(0)
        pl.semaphore_wait(barrier, greetings)
        fast_sends(0)

        def layer_step(layer, carry):
            slot = layer
            (shared,) = edges(layer, [shared_edge(slow)])
            put_shared(slot, slow, shared)
            z_faces(slot, middle, MID)
            starts(slot, MID)
            put(slot, slow, shared + inside(edges(layer, own_edges(slow))), False)
            z_faces(slot, [slow], SLOW)
            starts(slot, SLOW)

            arrivals(slot, FAST)
            columns = z_columns(slot, fast, FAST)
            keep_nodes(fast, node(layer, slot, fast, columns))

            @pl.when(layer + 1 < layers)
            def _():
                fast_edges(layer + 1)

            arrivals(slot, MID)
            columns = z_columns(slot, None, MID)
            for x in middle:
                keep_nodes(x, node(layer, slot, x, columns))

            @pl.when(layer + 1 < layers)
            def _():
                middle_edges(layer + 1)
                fast_sends(layer + 1)

            for message in messages:
                sent(message, layer, slow)
            arrivals(slot, SLOW)
            columns = z_columns(slot, slow, SLOW)
            keep_nodes(slow, node(layer, slot, slow, columns))
            return carry

        lax.fori_loop(0, layers, layer_step, 0)

    pl.when(lax.rem(place[0], 2) == 0)(lambda: run(0))
    pl.when(lax.rem(place[0], 2) == 1)(lambda: run(last))
    for x in range(cx):
        final = h_s[x].astype(F32)
        for y in range(cy):
            stage_s[x, pl.ds(y, chans, stride=cy), :] = at_y(final, y)
        out_ref[:, x] = stage_s[x].reshape(chans, cy, cz).astype(BF16)


def solution(mesh):
    sizes = tuple(mesh.shape[axis] for axis in AXES)

    def on_device(features, edge_state, multiplicity, *params):
        layers = params[0].shape[0]
        chans, cx, cy, cz = features.shape
        rows, cells = chans * cy, cy * cz
        assert cz == 128 and rows % 128 == 0 and cy % 8 == 0 and cx > 2
        assert chans % 16 == 0 and 128 % chans == 0 and cx * rows <= 64 * 128
        slots = layers
        ways = len(messages_of(sizes))
        zrows = -(-cx * (rows // 128) // 8) * 8
        vmem = pl.BlockSpec(memory_space=pltpu.VMEM)
        scratch = [pltpu.VMEM(a.shape, a.dtype) for a in (features, edge_state, multiplicity, *params)]
        scratch += [
            pltpu.VMEM((4 * cx, rows, cz), F32),
            pltpu.VMEM((cx, chans, cells), BF16),
            pltpu.VMEM((cx, chans, cells), BF16),
            pltpu.VMEM((3, cx, chans, cells), BF16),
            pltpu.VMEM((3, cx, 8, cells), F32),
            pltpu.VMEM((slots, cx, chans, cells), F32),
            pltpu.VMEM((layers, chans, cz), F32),
            pltpu.VMEM((layers, chans, cz), F32),
            pltpu.VMEM((slots, 2, 3, zrows, 128), F32),
            pltpu.VMEM((slots, 2, chans, cells), F32),
            pltpu.VMEM((slots, 2, cx, chans, cz), F32),
            pltpu.VMEM((slots, 4, chans, cz), F32),
            pltpu.VMEM((slots, 2, 5, 3, zrows, 128), F32),
            pltpu.VMEM((4, 128, 128), F32),
            pltpu.SemaphoreType.DMA((9,)),
            pltpu.SemaphoreType.DMA((slots, ways)),
            pltpu.SemaphoreType.DMA((slots, ways)),
        ]
        return pl.pallas_call(
            functools.partial(kernel, sizes, layers),
            out_shape=pltpu.VMEM(features.shape, features.dtype),
            in_specs=[pl.BlockSpec(memory_space=pltpu.HBM)] * 9,
            out_specs=vmem,
            scratch_shapes=scratch,
            compiler_params=pltpu.CompilerParams(
                collective_id=0, has_side_effects=True, vmem_limit_bytes=60 * 1024 * 1024
            ),
        )(features, edge_state, multiplicity, *params)

    placed = (P(None, *AXES), P(None, None, *AXES), P(*AXES)) + (P(),) * 6
    return jax.shard_map(
        on_device, mesh=mesh, in_specs=placed, out_specs=P(None, *AXES), check_vma=False
    )
```

```python
import functools
import itertools

import jax
import jax.numpy as jnp
from jax import lax
from jax.experimental import pallas as pl
from jax.experimental.pallas import tpu as pltpu
from jax.sharding import PartitionSpec as P

MESH = pl.DeviceIdType.MESH
AXES = ("gx", "gy", "gz")
F32, BF16 = jnp.float32, jnp.bfloat16
STEPS = (-1, 0, 1)
FAST, SLOW, MID = 0, 1, 2
OTHER = 2


def iota(shape, dim):
    return lax.broadcasted_iota(jnp.int32, shape, dim)


def dot(a, b):
    return jnp.dot(a, b, preferred_element_type=F32)


def silu_of_half(half):
    return half + half * jnp.tanh(half)


def ways_of(sizes):
    z_steps = {1: (0,), 2: (0, OTHER)}.get(sizes[2], STEPS)
    ways = itertools.product(STEPS, STEPS, z_steps)
    return [
        way for way in ways if any(way) and all(s == 0 or n > 1 for s, n in zip(way, sizes))
    ]


def messages_of(sizes):
    out = []
    for way in ways_of(sizes):
        dx, dy, dz = way
        out += [(way, tag) for tag in ((FAST, SLOW, MID) if dx == 0 else (None,))]
    return out


def kernel(
    sizes,
    layers,
    feat_hbm, edge_hbm, mult_hbm, win_hbm, wout_hbm, bin_hbm, nin_hbm, nout_hbm, bnode_hbm,
    out_ref,
    feat_ref, edge_ref, mult_ref, win_ref, wout_ref, bin_ref, nin_ref, nout_ref, bnode_ref,
    stage_s, h_s, hz_s, e_s, w_s, p_s, bias_e, bias_n,
    zsend, xrx, yrx, xyrx, zrx, turn_s, in_sem, send_sem, recv_sem,
):
    loads = [
        pltpu.make_async_copy(source, target, in_sem.at[index])
        for index, (source, target) in enumerate([
            (win_hbm, win_ref), (wout_hbm, wout_ref), (bin_hbm, bin_ref), (nin_hbm, nin_ref),
            (nout_hbm, nout_ref), (bnode_hbm, bnode_ref), (mult_hbm, mult_ref),
            (feat_hbm, feat_ref), (edge_hbm, edge_ref),
        ])
    ]
    for load in loads[::-1]:
        load.start()

    chans, cx, cy, cz = feat_ref.shape
    rows, cells = chans * cy, cy * cz
    halves = rows // 128
    per_half = cy // halves
    last = cx - 1
    zrows = zsend.shape[3]
    place = [lax.axis_index(axis) for axis in AXES]

    def exists(way):
        there = None
        for pos, step, size in zip(place, way, sizes):
            if step == 0 or step == OTHER:
                continue
            here = pos > 0 if step < 0 else pos < size - 1
            there = here if there is None else there & here
        return there

    def device(way):
        return {
            axis: 1 - pos if step == OTHER else pos + step
            for axis, pos, step in zip(AXES, place, way)
        }

    def back(way):
        return tuple(step if step == OTHER else -step for step in way)

    def when_exists(way, act):
        there = exists(way)
        if there is None:
            act()
        else:
            pl.when(there)(act)

    ways = ways_of(sizes)
    messages = messages_of(sizes)
    z_steps = [way[2] for way in ways if way[0] == 0 and way[1] == 0 and way[2] != 0]

    xrx[...] = jnp.zeros_like(xrx)
    yrx[...] = jnp.zeros_like(yrx)
    xyrx[...] = jnp.zeros_like(xyrx)
    zrx[...] = jnp.zeros_like(zrx)

    barrier = pltpu.get_barrier_semaphore()
    for way in sorted(ways, key=lambda way: -sum(step != 0 for step in way)):
        def greet(way=way):
            pl.semaphore_signal(barrier, inc=1, device_id=device(way), device_id_type=MESH)

        when_exists(way, greet)

    def at_y(values, y):
        return values[:, y * cz : (y + 1) * cz]

    def over_y(make):
        return jnp.concatenate([make(y) for y in range(cy)], axis=1)

    for load in loads[:7]:
        load.wait()
    diagonal = iota((chans, chans), 0) == iota((chans, chans), 1)
    for source, target in ((bin_ref, bias_e), (bnode_ref, bias_n)):
        for layer in range(layers):
            row = source[layer : layer + 1, :]
            column = jnp.sum(jnp.where(diagonal, row, 0.0), axis=1, keepdims=True)
            target[layer] = jnp.broadcast_to(0.5 * column, (chans, cz))

    def halved(weights):
        return (0.5 * weights.astype(F32)).astype(BF16)

    fluid = mult_ref[1, 1:2, 1:2] > 0
    zeros = jnp.zeros((cy, cz), jnp.int32)
    for x in range(cx):
        count = mult_ref[x]
        ahead = (
            mult_ref[x + 1] if x < last else zeros,
            jnp.where(iota((cy, cz), 0) < cy - 1, pltpu.roll(count, cy - 1, 0), 0),
            jnp.where(iota((cy, cz), 1) < cz - 1, pltpu.roll(count, cz - 1, 1), 0),
        )
        for d in range(3):
            shared = jnp.minimum(count, ahead[d])
            weight = jnp.where(
                fluid & (shared > 0), 1.0 / jnp.maximum(shared, 1).astype(F32), 0.0
            )
            w_s[d, x] = over_y(lambda y: jnp.broadcast_to(weight[y : y + 1], (8, cz)))

    before_end = iota((chans, cz), 1) < cz - 1

    def keep_nodes(x, values):
        h_s[x] = values.astype(BF16)
        hz_s[x] = over_y(
            lambda y: jnp.where(before_end, pltpu.roll(at_y(values, y), cz - 1, 1), 0.0)
        ).astype(BF16)

    def channel_rows(index, values):
        stage_s[index] = values.astype(F32).reshape(rows, cz)
        return over_y(lambda y: stage_s[index, pl.ds(y, chans, stride=cy), :])

    loads[7].wait()
    for x in range(cx):
        keep_nodes(x, channel_rows(x, feat_ref[:, x]))
    loads[8].wait()
    for x in range(cx):
        for d in range(3):
            index = (1 + d) * cx + x
            e_s[d, x] = channel_rows(index, edge_ref[d, :, x]).astype(BF16)

    def next_nodes(x, d):
        if d == 2:
            return hz_s[x]
        if d == 1:
            return jnp.concatenate([h_s[x][:, cz:], jnp.zeros((chans, cz), BF16)], axis=1)
        return h_s[x + 1] if x < last else jnp.zeros((chans, cells), BF16)

    def edges(layer, slabs):
        weight_in, weight_out = halved(win_ref[layer]), wout_ref[layer]
        bias = jnp.concatenate([bias_e[layer]] * cy, axis=1)
        weighted = []
        for x, d in slabs:
            edge = e_s[d, x]
            stacked = jnp.concatenate([h_s[x], next_nodes(x, d), edge], axis=0)
            half = dot(weight_in, stacked) + bias
            message = dot(weight_out, silu_of_half(half).astype(BF16))
            e_s[d, x] = (edge.astype(F32) + message).astype(BF16)
            spread = message.reshape(chans // 8, 8, cells) * w_s[d, x][None]
            weighted.append(spread.reshape(chans, cells))
        return weighted

    def both_y(weighted):
        return weighted + jnp.concatenate(
            [jnp.zeros((chans, cz), F32), weighted[:, : cells - cz]], axis=1
        )

    def both_z(weighted):
        return weighted + over_y(lambda y: pltpu.roll(at_y(weighted, y), 1, 1))

    def put(slot, x, value, add):
        p_s[slot, x] = p_s[slot, x] + value if add else value

    def edge_lanes(side):
        return pl.ds(0 if side == 0 else cells - cz, cz)

    def transfer(message, slot, slow):
        way, tag = message
        dx, dy, dz = way
        index = messages.index(message)
        side = 0 if dy < 0 else 1
        face = 0 if dx < 0 else last
        if dz != 0:
            which = z_steps.index(dz)
            source = zsend.at[slot, which, SLOW if tag is None and face == slow else tag or FAST]
            target = zrx.at[slot, which, {-1: 0, 0: 1 + (tag or 0), 1: 4}[dx], dy + 1]
        elif dy == 0:
            source = p_s.at[slot, face]
            target = xrx.at[slot, 0 if dx < 0 else 1]
        elif dx == 0:
            slabs = {FAST: (last - slow, 1), SLOW: (slow, 1), MID: (1, last - 1)}[tag]
            slabs = pl.ds(*slabs)
            source = p_s.at[slot, slabs, :, edge_lanes(side)]
            target = yrx.at[slot, side, slabs]
        else:
            source = p_s.at[slot, face, :, edge_lanes(side)]
            target = xyrx.at[slot, (0 if dx < 0 else 2) + side]
        return pltpu.make_async_remote_copy(
            src_ref=source,
            dst_ref=target,
            send_sem=send_sem.at[slot, index],
            recv_sem=recv_sem.at[slot, index],
            device_id=device(way),
            device_id_type=MESH,
        )

    def start(message, slot, slow):
        when_exists(message[0], lambda: transfer(message, slot, slow).start())

    def arrive(message, slot, slow):
        when_exists(back(message[0]), lambda: transfer(message, slot, slow).wait_recv())

    def sent(message, slot, slow):
        when_exists(message[0], lambda: transfer(message, slot, slow).wait_send())

    lane = iota((128, cz), 1)
    odd_rows, even_rows = pl.ds(1, zrows, stride=2), pl.ds(0, zrows, stride=2)

    def z_faces(slot, xs, phase):
        faces = jnp.zeros((128, cz), F32)
        for x in xs:
            for part in range(halves):
                at = 2 * (x * halves + part)
                whole = p_s[slot, x]
                piece = jnp.concatenate(
                    [at_y(whole, part * per_half + y) for y in range(per_half)], axis=0
                )
                piece = pltpu.roll(piece, at + 1, 1)
                faces = jnp.where((lane == at) | (lane == at + 1), piece, faces)
        turn_s[3] = faces.T
        first, final = turn_s[3, odd_rows, :], turn_s[3, even_rows, :]
        for which, dz in enumerate(z_steps):
            if dz == OTHER:
                zsend[slot, which, phase] = jnp.where(place[2] == 0, final, first)
            else:
                zsend[slot, which, phase] = first if dz < 0 else final

    row_z, lane_z = iota((zrows, 128), 0), iota((zrows, 128), 1)

    def z_total(slot, which, face, phase):
        total = jnp.zeros((zrows, 128), F32)
        shift_x = last * halves
        for dy in STEPS:
            part = zrx[slot, which, 1 + phase, dy + 1]
            piece = 0.0
            if face == 0:
                piece = zrx[slot, which, 4, dy + 1]
                piece = jnp.where(row_z < halves, pltpu.roll(piece, zrows - shift_x, 0), 0.0)
            elif face == last:
                piece = zrx[slot, which, 0, dy + 1]
                inside = (row_z >= shift_x) & (row_z < shift_x + halves)
                piece = jnp.where(inside, pltpu.roll(piece, shift_x, 0), 0.0)
            part = part + piece
            if dy > 0:
                part = pltpu.roll(pltpu.roll(part, chans % 128, 1), zrows - halves + 1, 0)
                part = jnp.where((row_z % halves == 0) & (lane_z < chans), part, 0.0)
            if dy < 0:
                part = pltpu.roll(pltpu.roll(part, 128 - chans, 1), halves - 1, 0)
                inside = (row_z % halves == halves - 1) & (lane_z >= 128 - chans)
                part = jnp.where(inside, part, 0.0)
            total = total + part
        return total

    def z_columns(slot, face, phase):
        for which, dz in enumerate(z_steps):
            total = z_total(slot, which, face, phase)
            if dz != 1:
                turn_s[phase, even_rows, :] = jnp.where(place[2] < sizes[2] - 1, total, 0.0)
            if dz != -1:
                turn_s[phase, odd_rows, :] = jnp.where(place[2] > 0, total, 0.0)
        return turn_s[phase].T

    def z_add(columns, x):
        out = []
        for part in range(halves):
            at = 2 * (x * halves + part)
            piece = pltpu.roll(columns, cz - at - 1, 1)
            out.append(jnp.where((lane == 0) | (lane == cz - 1), piece, 0.0))
        return over_y(
            lambda y: out[y // per_half][y % per_half * chans : (y % per_half + 1) * chans]
        )

    def node(layer, slot, x, columns):
        total = p_s[slot, x] + z_add(columns, x)
        if x == 0:
            total = total + xrx[slot, 1]
        if x == last:
            total = total + xrx[slot, 0]
        blocks = [at_y(total, y) for y in range(cy)]
        for side in range(2):
            extra = yrx[slot, 1 - side, x]
            if x == 0:
                extra = extra + xyrx[slot, 2 + (1 - side)]
            if x == last:
                extra = extra + xyrx[slot, 1 - side]
            blocks[-side] = blocks[-side] + extra
        incoming = jnp.concatenate(blocks, axis=1).astype(BF16)
        stacked = jnp.concatenate([h_s[x], incoming], axis=0)
        half = dot(halved(nin_ref[layer]), stacked)
        half = half + jnp.concatenate([bias_n[layer]] * cy, axis=1)
        step = dot(nout_ref[layer], silu_of_half(half).astype(BF16))
        return (h_s[x].astype(F32) + step).astype(BF16).astype(F32)

    turn_s[...] = jnp.zeros_like(turn_s)
    greetings = -1 + functools.reduce(
        lambda a, b: a * b,
        [
            1 + (pos > 0).astype(jnp.int32) + (pos < size - 1).astype(jnp.int32)
            for pos, size in zip(place, sizes)
        ],
    )
    middle = list(range(1, last))

    def run(slow):
        fast = last - slow

        def phase_of(message, sending):
            (dx, dy, dz), tag = message
            if dx != 0:
                face = 0 if (dx < 0) == sending else last
                return FAST if face == fast else SLOW
            return tag

        def order(message):
            (dx, dy, dz), tag = message
            hops = sum(step != 0 for step in (dx, dy, dz))
            return (dz == 0, dz == 0 and dy != 0, -hops)

        ordered = sorted(messages, key=order)

        def starts(slot, phase):
            for message in ordered:
                if phase_of(message, True) == phase:
                    start(message, slot, slow)

        def arrivals(slot, phase):
            for message in ordered:
                if phase_of(message, False) == phase:
                    arrive(message, slot, slow)

        def shared_edge(face):
            return (0 if face == 0 else last - 1, 0)

        def own_edges(face):
            return ([(last, 0)] if face == last else []) + [(face, 2), (face, 1)]

        def inside(weighted):
            *absent, wz, wy = weighted
            return sum(absent, both_z(wz) + both_y(wy))

        def put_shared(slot, face, shared):
            put(slot, 1 if face == 0 else last - 1, shared, True)

        def fast_edges(layer):
            put(layer, fast, inside(edges(layer, own_edges(fast))), False)

        def middle_edges(layer):
            inner = [(x, 0) for x in middle[:-1]]
            for x in middle:
                put(layer, x, inside(edges(layer, [(x, 2), (x, 1)])), False)
            shared, *weighted = edges(layer, [shared_edge(fast)] + inner)
            for (x, d), value in zip(inner, weighted):
                put(layer, x, value, True)
                put(layer, x + 1, value, True)
            put(layer, fast, shared, True)
            put_shared(layer, fast, shared)

        def fast_sends(slot):
            z_faces(slot, [fast], FAST)
            starts(slot, FAST)

        fast_edges(0)
        middle_edges(0)
        pl.semaphore_wait(barrier, greetings)
        fast_sends(0)

        def layer_step(layer, carry):
            slot = layer
            (shared,) = edges(layer, [shared_edge(slow)])
            put_shared(slot, slow, shared)
            z_faces(slot, middle, MID)
            starts(slot, MID)
            put(slot, slow, shared + inside(edges(layer, own_edges(slow))), False)
            z_faces(slot, [slow], SLOW)
            starts(slot, SLOW)

            arrivals(slot, FAST)
            columns = z_columns(slot, fast, FAST)
            keep_nodes(fast, node(layer, slot, fast, columns))

            @pl.when(layer + 1 < layers)
            def _():
                fast_edges(layer + 1)

            arrivals(slot, MID)
            columns = z_columns(slot, None, MID)
            for x in middle:
                keep_nodes(x, node(layer, slot, x, columns))

            @pl.when(layer + 1 < layers)
            def _():
                middle_edges(layer + 1)
                fast_sends(layer + 1)

            for message in messages:
                sent(message, layer, slow)
            arrivals(slot, SLOW)
            columns = z_columns(slot, slow, SLOW)
            keep_nodes(slow, node(layer, slot, slow, columns))
            return carry

        lax.fori_loop(0, layers, layer_step, 0)

    pl.when(lax.rem(place[0], 2) == 0)(lambda: run(0))
    pl.when(lax.rem(place[0], 2) == 1)(lambda: run(last))
    for x in range(cx):
        final = h_s[x].astype(F32)
        for y in range(cy):
            stage_s[x, pl.ds(y, chans, stride=cy), :] = at_y(final, y)
        out_ref[:, x] = stage_s[x].reshape(chans, cy, cz).astype(BF16)


def solution(mesh):
    sizes = tuple(mesh.shape[axis] for axis in AXES)

    def on_device(features, edge_state, multiplicity, *params):
        layers = params[0].shape[0]
        chans, cx, cy, cz = features.shape
        rows, cells = chans * cy, cy * cz
        assert cz == 128 and rows % 128 == 0 and cy % 8 == 0 and cx > 2
        assert chans % 16 == 0 and 128 % chans == 0 and cx * rows <= 64 * 128
        slots = layers
        ways = len(messages_of(sizes))
        zrows = -(-cx * (rows // 128) // 8) * 8
        vmem = pl.BlockSpec(memory_space=pltpu.VMEM)
        scratch = [pltpu.VMEM(a.shape, a.dtype) for a in (features, edge_state, multiplicity, *params)]
        scratch += [
            pltpu.VMEM((4 * cx, rows, cz), F32),
            pltpu.VMEM((cx, chans, cells), BF16),
            pltpu.VMEM((cx, chans, cells), BF16),
            pltpu.VMEM((3, cx, chans, cells), BF16),
            pltpu.VMEM((3, cx, 8, cells), F32),
            pltpu.VMEM((slots, cx, chans, cells), F32),
            pltpu.VMEM((layers, chans, cz), F32),
            pltpu.VMEM((layers, chans, cz), F32),
            pltpu.VMEM((slots, 2, 3, zrows, 128), F32),
            pltpu.VMEM((slots, 2, chans, cells), F32),
            pltpu.VMEM((slots, 2, cx, chans, cz), F32),
            pltpu.VMEM((slots, 4, chans, cz), F32),
            pltpu.VMEM((slots, 2, 5, 3, zrows, 128), F32),
            pltpu.VMEM((4, 128, 128), F32),
            pltpu.SemaphoreType.DMA((9,)),
            pltpu.SemaphoreType.DMA((slots, ways)),
            pltpu.SemaphoreType.DMA((slots, ways)),
        ]
        return pl.pallas_call(
            functools.partial(kernel, sizes, layers),
            out_shape=pltpu.VMEM(features.shape, features.dtype),
            in_specs=[pl.BlockSpec(memory_space=pltpu.HBM)] * 9,
            out_specs=vmem,
            scratch_shapes=scratch,
            compiler_params=pltpu.CompilerParams(
                collective_id=0, has_side_effects=True, vmem_limit_bytes=60 * 1024 * 1024
            ),
        )(features, edge_state, multiplicity, *params)

    placed = (P(None, *AXES), P(None, None, *AXES), P(*AXES)) + (P(),) * 6
    return jax.shard_map(
        on_device, mesh=mesh, in_specs=placed, out_specs=P(None, *AXES), check_vma=False
    )
```
